128 devices in a mesh: order: 4 (over z), shard: 32 (over x, y, core).
Axes of the slice: x: 4, y: 4, z: 4, core: 2. Of those that a mesh axis runs over, the one named last changes fastest.
Arguments:
- sky_coeffs: float32 [32, 2, 2048], P('shard'), may hold values from -6 to 6
- beam_coeffs: float32 [64, 2048], P('order'), may hold values from -0.09375 to 0.09375
- wigner: bfloat16 [32, 64, 2048, 128], P('shard', 'order'), may hold values from -0.125 to 0.125
- visits: int32 [128, 128, 4], P(('order', 'shard')), may hold values from -1 to 127, as said below
- point_slot: int32 [2097152], P(('order', 'shard')), may hold values from 0 to 511, as said below
- phi_cell: int32 [2097152], P(('order', 'shard')), may hold values from 0 to 30
- psi_cell: int32 [2097152], P(('order', 'shard')), may hold values from 0 to 127
- fraction: float32 [2, 2097152], P(None, ('order', 'shard')), may hold values from 0 to 1
Outputs:
- timeline: float32 [2097152], P(('order', 'shard'))
The draws below stay inside these ranges and needn't reach their ends.
Inputs may be any that keep to these rules, and one draw needn't show every extreme that they name: Live entries of one row visits[r, d] are distinct tiles of owner d and come first; every row holds 1 to 4 live entries; for every device r some owner d has all 4 entries live. `point_slot`: every pointing names a live entry of its own device's visit list. Of one device's pointings, exactly 192 name each of half of the owners and 64 each of the others.
All inputs are finite; a program needn't handle non-finite values.
Results may differ from the reference program's by a relative error of at most 0.008.
Values may be sent and summed in bfloat16 or wider, within the bound.
No kernel may reach another device: no remote copies, remote signals or barrier semaphores. Data moves between devices by JAX's collectives and lax.ppermute only.
A program may use at most 64 MiB of HBM per device.

```python
import math
import jax
import jax.numpy as jnp
from jax import lax

L = 2048
KBEAM = 64
NPHI = 4096
NPSI = 128
PHI_T = 32
SLOTS = 4
ROWS = 4
P_DEV = 16384
MTOT = 32
THETA = 128
PTOT = 2097152
BLOCKS = 32
TPO = 128
N_ORDER = 4
N_SHARD = 32
DEVICES = 128


def visit_plan(key):
    base = jax.random.fold_in(key, 7)
    key_count, key_score, key_full = jax.random.split(base, 3)
    counts = jax.random.randint(key_count, (DEVICES, DEVICES), 1, SLOTS + 1)
    full_owner = jax.random.permutation(key_full, DEVICES)
    owners = jnp.arange(DEVICES, dtype=jnp.int32)[None, :]
    counts = jnp.where(owners == full_owner[:, None], SLOTS, counts)
    scores = jax.random.randint(key_score, (DEVICES, DEVICES, TPO), 0, 1048576) * TPO
    scores = scores + jnp.arange(TPO, dtype=jnp.int32)[None, None, :]
    picked = jnp.argsort(scores, axis=-1)[:, :, :SLOTS].astype(jnp.int32)
    live = jnp.arange(SLOTS, dtype=jnp.int32)[None, None, :] < counts[:, :, None]
    return (jnp.where(live, picked, -1).astype(jnp.int32), counts.astype(jnp.int32))


def draw_visits(key, part):
    table, counts = visit_plan(key)
    return table


def draw_point_slot(key, part):
    table, counts = visit_plan(key)
    key_perm, key_order, key_slot = jax.random.split(jax.random.fold_in(key, 11), 3)
    per_owner = P_DEV // DEVICES
    half = P_DEV // 2
    position = jnp.arange(P_DEV, dtype=jnp.int32)
    light = position % DEVICES
    heavy = (position - half) // per_owner
    rank_owner = jnp.where(position < half, light, heavy).astype(jnp.int32)
    perm_scores = jax.random.randint(key_perm, (DEVICES, DEVICES), 0, 65536) * DEVICES
    perm_scores = perm_scores + jnp.arange(DEVICES, dtype=jnp.int32)[None, :]
    owner_perm = jnp.argsort(perm_scores, axis=-1).astype(jnp.int32)
    owner_base = owner_perm[:, rank_owner]
    order_scores = jax.random.randint(key_order, (DEVICES, P_DEV), 0, 8192) * P_DEV
    order_scores = order_scores + position[None, :]
    shuffle = jnp.argsort(order_scores, axis=-1).astype(jnp.int32)
    owner = jnp.take_along_axis(owner_base, shuffle, axis=1).reshape(PTOT).astype(jnp.int32)
    device = jnp.arange(PTOT, dtype=jnp.int32) // P_DEV
    live_count = counts[device, owner]
    slot = jax.random.randint(key_slot, (PTOT,), 0, 65536) * live_count // 65536
    return (owner * SLOTS + slot).astype(jnp.int32)


def touch_ends(result, stream_key, least, top_value):
    place = [jax.random.randint(jax.random.fold_in(stream_key, axis), (), 0, length) for axis, length in enumerate(result.shape)]
    longest = result.shape.index(max(result.shape))
    next_to = place[:longest] + [(place[longest] + 1) % result.shape[longest]] + place[longest + 1:]
    return result.at[tuple(place)].set(least).at[tuple(next_to)].set(top_value)


def shard_levels(key, extent, shards, low, high):
    loudness = 1.0
    for axis_at, parts in shards:
        steps = jax.random.uniform(jax.random.fold_in(jax.random.fold_in(key, 6), axis_at), (parts,), jnp.float32, low / len(shards), high / len(shards))
        loudness = loudness * jnp.repeat(jnp.exp(steps), extent[axis_at] // parts).reshape((-1,) + (1,) * (len(extent) - 1 - axis_at))
    return loudness


def bell_draw(rng, dims, width, limit, shards=(), kind=jnp.bfloat16):
    result = width * jax.random.normal(rng, dims, jnp.float32)
    if shards:
        result = result * shard_levels(rng, dims, shards, -0.22, 0.18)
    return jnp.clip(result, -limit, limit).astype(kind)


def setup_inputs(seed: int = 0) -> dict:
    splits = jax.random.split(jax.random.key(seed), 9)
    sky_coeffs = bell_draw(splits[0], (MTOT, 2, L), 1.0, 6.0, ((0, 32),), jnp.float32)
    beam_coeffs = bell_draw(splits[1], (KBEAM, L), (2 * MTOT * KBEAM) ** -0.5, 0.09375, ((0, 4),), jnp.float32)
    wigner = bell_draw(splits[2], (MTOT, KBEAM, L, THETA), L ** -0.5, 0.125, ((0, 32), (1, 4)))
    visits = draw_visits(jax.random.fold_in(splits[8], 71), 0)
    point_slot = draw_point_slot(jax.random.fold_in(splits[8], 71), 0)
    phi_cell = touch_ends(jax.random.randint(splits[5], (PTOT,), 0, PHI_T - 1), jax.random.fold_in(splits[5], 1), 0, (PHI_T - 1) - 1).astype(jnp.int32)
    psi_cell = touch_ends(jax.random.randint(splits[6], (PTOT,), 0, NPSI), jax.random.fold_in(splits[6], 1), 0, NPSI - 1).astype(jnp.int32)
    fraction = jnp.clip(1.0 * jax.random.uniform(splits[7], (2, PTOT), jnp.float32) ** shard_levels(splits[7], (2, PTOT), ((1, 128),), -0.2, 0.2), 0.0, 1.0)
    return {"sky_coeffs": sky_coeffs, "beam_coeffs": beam_coeffs, "wigner": wigner, "visits": visits, "point_slot": point_slot, "phi_cell": phi_cell, "psi_cell": psi_cell, "fraction": fraction}


def wave_table(count, modes, first):
    grid = jnp.arange(count, dtype=jnp.int32)[:, None]
    mode = jnp.arange(modes, dtype=jnp.int32)[None, :] + first
    phase = ((grid * mode) % count).astype(jnp.float32) * (2.0 * math.pi / count)
    return jnp.cos(phase).astype(jnp.bfloat16), jnp.sin(phase).astype(jnp.bfloat16)


def reference(sky_coeffs, beam_coeffs, wigner, visits, point_slot, phi_cell, psi_cell, fraction):
    def mode_terms(pair):
        sky_mode, table_mode = pair
        weighted = (sky_mode[None, :, :] * beam_coeffs[:, None, :]).astype(jnp.bfloat16)
        terms = jnp.einsum("kcl,klt->tkc", weighted.astype(jnp.float32), table_mode.astype(jnp.float32))
        return terms.astype(jnp.bfloat16)

    coeffs = lax.map(mode_terms, (sky_coeffs, wigner))
    coeffs = jnp.transpose(coeffs, (1, 0, 2, 3))
    cos_phi, sin_phi = wave_table(NPHI, MTOT, 0)
    cos_psi, sin_psi = wave_table(NPSI, KBEAM, 0)
    group_orders = KBEAM // N_ORDER
    cos_group = jnp.transpose(cos_psi).reshape(N_ORDER, group_orders, NPSI).astype(jnp.float32)
    sin_group = jnp.transpose(sin_psi).reshape(N_ORDER, group_orders, NPSI).astype(jnp.float32)

    def theta_row(row):
        real_part = row[:, :, 0]
        imag_part = row[:, :, 1]
        synth_real = (jnp.dot(cos_phi, real_part, preferred_element_type=jnp.float32)
                      - jnp.dot(sin_phi, imag_part, preferred_element_type=jnp.float32)).astype(jnp.bfloat16)
        synth_imag = (jnp.dot(sin_phi, real_part, preferred_element_type=jnp.float32)
                      + jnp.dot(cos_phi, imag_part, preferred_element_type=jnp.float32)).astype(jnp.bfloat16)
        grouped_real = synth_real.reshape(NPHI, N_ORDER, group_orders).astype(jnp.float32)
        grouped_imag = synth_imag.reshape(NPHI, N_ORDER, group_orders).astype(jnp.float32)
        partial_value = (jnp.einsum("pok,okq->opq", grouped_real, cos_group)
                   - jnp.einsum("pok,okq->opq", grouped_imag, sin_group))
        rounded = lax.optimization_barrier(partial_value.astype(jnp.bfloat16)).astype(jnp.float32)
        return jnp.sum(rounded, axis=0).astype(jnp.bfloat16)

    cube = lax.map(theta_row, coeffs)
    flat_cube = cube.reshape(-1)
    device = (jnp.arange(PTOT, dtype=jnp.int32) // P_DEV).astype(jnp.int32)
    owner = point_slot // SLOTS
    tile = visits[device, owner, point_slot % SLOTS]
    owner_order = owner // N_SHARD
    owner_shard = owner % N_SHARD
    row_index = owner_shard * ROWS + tile // BLOCKS
    phi_index = owner_order * (NPHI // N_ORDER) + (tile % BLOCKS) * PHI_T + phi_cell
    next_psi = (psi_cell + 1) % NPSI
    base = row_index * (NPHI * NPSI) + phi_index * NPSI
    corner_aa = flat_cube[base + psi_cell].astype(jnp.float32)
    corner_ab = flat_cube[base + next_psi].astype(jnp.float32)
    corner_ba = flat_cube[base + NPSI + psi_cell].astype(jnp.float32)
    corner_bb = flat_cube[base + NPSI + next_psi].astype(jnp.float32)
    along_phi = fraction[0]
    along_psi = fraction[1]
    return ((1.0 - along_phi) * ((1.0 - along_psi) * corner_aa + along_psi * corner_ab)
            + along_phi * ((1.0 - along_psi) * corner_ba + along_psi * corner_bb))
```

```python
import math

import jax
import jax.numpy as jnp
import numpy as np
from jax import lax
from jax.experimental import pallas as pl
from jax.experimental.pallas import tpu as pltpu
from jax.sharding import PartitionSpec as P

BF = jnp.bfloat16
F32 = jnp.float32
MESH_AXES = ("order", "shard")
NPHI = 4096
NPSI = 128
MODES = 32
ORDERS = 64
GROUPS = 4
SHARDS = 32
OWNERS = 128
LANES = 128
RANKS = 256
ITEMS = 6
NT = (((1,), (1,)), ((), ()))


def phi_tables():
    phi = np.arange(NPHI, dtype=np.int64)[:, None]
    mode = np.arange(MODES, dtype=np.int64)[None, :]
    phase = ((phi * mode) % NPHI).astype(np.float64) * (2.0 * math.pi / NPHI)
    both = np.concatenate([np.cos(phase), -np.sin(phase)], axis=1)
    blocks = both.reshape(NPHI // 32, 32, 2 * MODES).transpose(0, 2, 1)
    return np.tile(blocks, (1, 1, 4)).astype(jnp.bfloat16)


def psi_tables():
    psi = np.arange(NPSI, dtype=np.int64)[:, None]
    order = np.arange(ORDERS, dtype=np.int64)[None, :]
    phase = ((psi * order) % NPSI).astype(np.float64) * (2.0 * math.pi / NPSI)
    cos, sin = np.cos(phase), np.sin(phase)
    real = np.stack([cos, -sin], axis=2).reshape(NPSI, 2 * ORDERS)
    imag = np.stack([sin, cos], axis=2).reshape(NPSI, 2 * ORDERS)
    return np.concatenate([real, imag], axis=0).astype(jnp.bfloat16)


def bucket_kernel(slot_ref, phi_ref, psi_ref, frac_ref, g_ref, rank_ref, carry, lhs, hot):
    own_iota = lax.broadcasted_iota(jnp.int32, (OWNERS, LANES), 0)
    rank_iota = lax.broadcasted_iota(jnp.int32, (RANKS, LANES), 0)
    before = (
        lax.broadcasted_iota(jnp.int32, (LANES, 2 * LANES), 0)
        < lax.broadcasted_iota(jnp.int32, (LANES, 2 * LANES), 1)
    ).astype(F32).astype(BF)
    carry[...] = jnp.zeros_like(carry)
    g_ref[...] = jnp.zeros_like(g_ref)

    def block(step, _):
        start = pl.multiple_of(step * 8, 8)
        slots = slot_ref[pl.ds(start, 8), :]
        owners = slots >> 2
        rows = ((slots & 3) * 32 + phi_ref[pl.ds(start, 8), :]).astype(F32)
        psis = psi_ref[pl.ds(start, 8), :].astype(F32)
        a = frac_ref[0, pl.ds(start, 8), :]
        b = frac_ref[1, pl.ds(start, 8), :]
        a_hi = a.astype(BF).astype(F32)
        b_hi = b.astype(BF).astype(F32)
        items = (rows, psis, a_hi, a - a_hi, b_hi, b - b_hi)
        seen = carry[...]
        ranks = []
        for u in range(8):
            mask = own_iota == owners[u : u + 1]
            hot_own = jnp.where(mask, 1.0, 0.0).astype(BF)
            count = jnp.dot(hot_own, before, preferred_element_type=F32)
            place = count[:, :LANES] + seen
            seen = seen + count[:, LANES:]
            rank = jnp.sum(jnp.where(mask, place, 0.0), axis=0, keepdims=True)
            ranks.append(rank)
            hot[:, u * LANES : (u + 1) * LANES] = jnp.where(
                rank_iota == rank.astype(jnp.int32), 1.0, 0.0
            ).astype(BF)
            for n, item in enumerate(items):
                lhs[n * OWNERS : (n + 1) * OWNERS, u * LANES : (u + 1) * LANES] = jnp.where(
                    mask, item[u : u + 1], 0.0
                ).astype(BF)
        carry[...] = seen
        rank_ref[pl.ds(start, 8), :] = jnp.concatenate(ranks, axis=0)
        g_ref[...] += lax.dot_general(lhs[...], hot[...], NT, preferred_element_type=F32)
        return 0

    lax.fori_loop(0, 16, block, 0)


def eval_kernel(
    visits_ref, coeff_ref, w_ref, phi_ref, g_ref, slot_ref, rank_ref, out_ref, coeff, found, pair
):
    def widen(step, _):
        start = pl.multiple_of(step * 128, 128)
        coeff[pl.ds(start, 128), :] = coeff_ref[pl.ds(start, 128), :].astype(F32)
        return 0

    lax.fori_loop(0, 32, widen, 0)
    lane = lax.broadcasted_iota(jnp.int32, (1, LANES), 1) // 32
    row_iota = lax.broadcasted_iota(jnp.int32, (LANES, RANKS), 0)

    def shard(s, _):
        block = coeff[pl.ds(s, 128, stride=SHARDS), :]
        turned = [block] + [pltpu.roll(block, 32 * n, axis=1) for n in (1, 2, 3)]
        rows = []
        for row in range(4):
            part = None
            for o in range(4):
                piece = turned[(o - row) % 4][o * 32 : (o + 1) * 32]
                part = piece if part is None else jnp.where(lane == o, piece, part)
            rows.append(part)
        block = jnp.concatenate(rows, axis=0).astype(BF)
        both = lax.dot_general(w_ref[...], block, NT, preferred_element_type=F32).astype(BF)
        both = jnp.concatenate([both[:NPSI], both[NPSI:]], axis=1)
        for o in range(4):
            d = o * SHARDS + s
            waves, lane_row = None, None
            for j in range(4):
                tile = jnp.maximum(visits_ref[d * 4 + j], 0)
                wave = phi_ref[o * 32 + (tile & 31)]
                row = jnp.full((1, LANES), tile >> 5, jnp.int32)
                waves = wave if j == 0 else jnp.where(lane == j, wave, waves)
                lane_row = row if j == 0 else jnp.where(lane == j, row, lane_row)
            parts = []
            for c in range(2):
                for row in range(4):
                    parts.append(
                        jnp.where(lane_row == row, waves[c * 32 : (c + 1) * 32], jnp.zeros((), BF))
                    )
            chosen = jnp.concatenate(parts, axis=0)
            tiles = jnp.dot(both, chosen, preferred_element_type=F32).astype(BF)
            at = [g_ref[pl.ds(n * OWNERS + d, 1), :] for n in range(ITEMS)]
            row0 = at[0].astype(jnp.int32)
            q0 = at[1].astype(jnp.int32)
            q1 = (q0 + 1) & (NPSI - 1)
            a = at[2] + at[3]
            b = at[4] + at[5]
            one_a = 1.0 - a
            lo = one_a.astype(BF).astype(F32)
            hi = a.astype(BF).astype(F32)
            on0 = row_iota == row0
            on1 = row_iota == row0 + 1
            main = jnp.where(on0, lo, jnp.where(on1, hi, 0.0)).astype(BF)
            rest = jnp.where(on0, one_a - lo, jnp.where(on1, a - hi, 0.0)).astype(BF)
            seen = jnp.dot(
                jnp.concatenate([tiles, tiles], axis=1),
                jnp.concatenate([main, rest], axis=0),
                preferred_element_type=F32,
            )
            weight = jnp.where(row_iota == q0, 1.0 - b, jnp.where(row_iota == q1, b, 0.0))
            found[pl.ds(d, 1), :] = jnp.sum(seen * weight, axis=0, keepdims=True)
        return 0

    lax.fori_loop(0, SHARDS, shard, 0)

    value = found[...]
    high = value.astype(BF)
    pair[:OWNERS, :] = high
    pair[OWNERS:, :] = (value - high.astype(F32)).astype(BF)
    own_iota = lax.broadcasted_iota(jnp.int32, (OWNERS, LANES), 0)
    rank_iota = lax.broadcasted_iota(jnp.int32, (RANKS, LANES), 0)

    def back(step, _):
        start = pl.multiple_of(step * 8, 8)
        owners = slot_ref[pl.ds(start, 8), :] >> 2
        ranks = rank_ref[pl.ds(start, 8), :].astype(jnp.int32)
        result = []
        for u in range(0, 8, 2):
            hot = jnp.concatenate(
                [
                    jnp.where(rank_iota == ranks[v : v + 1], 1.0, 0.0).astype(BF)
                    for v in (u, u + 1)
                ],
                axis=1,
            )
            moved = jnp.dot(pair[...], hot, preferred_element_type=F32)
            moved = moved[:OWNERS] + moved[OWNERS:]
            for v in (u, u + 1):
                part = moved[:, (v - u) * LANES : (v - u + 1) * LANES]
                result.append(
                    jnp.sum(
                        jnp.where(own_iota == owners[v : v + 1], part, 0.0), axis=0, keepdims=True
                    )
                )
        out_ref[pl.ds(start, 8), :] = jnp.concatenate(result, axis=0)
        return 0

    lax.fori_loop(0, 16, back, 0)


def shards(sky_coeffs, beam_coeffs, wigner, visits, point_slot, phi_cell, psi_cell, fraction):
    weighted = (sky_coeffs[0][None, :, :] * beam_coeffs[:, None, :]).astype(BF)
    coeffs = jnp.einsum("kcl,klt->tkc", weighted, wigner[0], preferred_element_type=F32)
    coeffs = coeffs.astype(BF).reshape(SHARDS, LANES)
    everyone = lax.all_to_all(
        jnp.broadcast_to(coeffs[None], (OWNERS, SHARDS, LANES)), MESH_AXES, 0, 0, tiled=True
    )
    slots = point_slot.reshape(OWNERS, LANES)
    cells = phi_cell.reshape(OWNERS, LANES)
    psis = psi_cell.reshape(OWNERS, LANES)
    fractions = fraction.reshape(2, OWNERS, LANES)
    vmem = pl.BlockSpec(memory_space=pltpu.VMEM)
    grouped, ranks = pl.pallas_call(
        bucket_kernel,
        out_shape=(
            jax.ShapeDtypeStruct((ITEMS * OWNERS, RANKS), F32),
            jax.ShapeDtypeStruct((OWNERS, LANES), F32),
        ),
        in_specs=[vmem] * 4,
        out_specs=(vmem, vmem),
        scratch_shapes=[
            pltpu.VMEM((OWNERS, LANES), F32),
            pltpu.VMEM((ITEMS * OWNERS, 1024), BF),
            pltpu.VMEM((RANKS, 1024), BF),
        ],
        compiler_params=pltpu.CompilerParams(vmem_limit_bytes=24 * 1024 * 1024),
        cost_estimate=pl.CostEstimate(
            flops=8 * 1024**3, bytes_accessed=2 * 1024**2, transcendentals=0
        ),
        name="bucket",
    )(slots, cells, psis, fractions)
    timeline = pl.pallas_call(
        eval_kernel,
        out_shape=jax.ShapeDtypeStruct((OWNERS, LANES), F32),
        in_specs=[pl.BlockSpec(memory_space=pltpu.SMEM)] + [vmem] * 6,
        out_specs=vmem,
        scratch_shapes=[
            pltpu.VMEM((OWNERS * SHARDS, LANES), F32),
            pltpu.VMEM((OWNERS, RANKS), F32),
            pltpu.VMEM((2 * OWNERS, RANKS), BF),
        ],
        compiler_params=pltpu.CompilerParams(vmem_limit_bytes=32 * 1024 * 1024),
        name="evaluate",
    )(
        visits.reshape(-1),
        everyone.reshape(OWNERS * SHARDS, LANES),
        jnp.asarray(psi_tables()),
        jnp.asarray(phi_tables()),
        grouped,
        slots,
        ranks,
    )
    return timeline.reshape(-1)


def solution(mesh):
    placed = (
        P("shard", None, None),
        P("order", None),
        P("shard", "order", None, None),
        P(("order", "shard"), None, None),
        P(("order", "shard")),
        P(("order", "shard")),
        P(("order", "shard")),
        P(None, ("order", "shard")),
    )
    return jax.shard_map(
        shards, mesh=mesh, in_specs=placed, out_specs=P(("order", "shard")), check_vma=False
    )
```

```python
import math

import jax
import jax.numpy as jnp
import numpy as np
from jax import lax
from jax.experimental import pallas as pl
from jax.experimental.pallas import tpu as pltpu
from jax.sharding import PartitionSpec as P

BF = jnp.bfloat16
F32 = jnp.float32
MESH_AXES = ("order", "shard")
NPHI = 4096
NPSI = 128
MODES = 32
ORDERS = 64
GROUPS = 4
SHARDS = 32
OWNERS = 128
LANES = 128
RANKS = 192
WIDE = 256
ITEMS = 4
LOCAL = 16
DEGREES = 2048
REPEAT = 16
MIB = 1024 * 1024
NT = (((1,), (1,)), ((), ()))


def phi_tables():
    phi = np.arange(NPHI, dtype=np.int64)[:, None]
    mode = np.arange(MODES, dtype=np.int64)[None, :]
    phase = ((phi * mode) % NPHI).astype(np.float64) * (2.0 * math.pi / NPHI)
    both = np.concatenate([np.cos(phase), -np.sin(phase)], axis=1)
    blocks = both.reshape(NPHI // 32, 32, 2 * MODES).transpose(0, 2, 1)
    return np.tile(blocks, (1, 1, 4)).astype(jnp.bfloat16)


def psi_tables():
    psi = np.arange(NPSI, dtype=np.int64)[:, None]
    order = np.arange(ORDERS, dtype=np.int64)[None, :]
    phase = ((psi * order) % NPSI).astype(np.float64) * (2.0 * math.pi / NPSI)
    cos, sin = np.cos(phase), np.sin(phase)
    real = np.stack([cos, -sin], axis=2).reshape(NPSI, 2 * ORDERS)
    imag = np.stack([sin, cos], axis=2).reshape(NPSI, 2 * ORDERS)
    return np.concatenate([real, imag], axis=0).astype(jnp.bfloat16)


def iota_bf(shape, dim):
    return lax.broadcasted_iota(jnp.int32, shape, dim).astype(F32).astype(BF)


def coeff_kernel(
    sky_hbm, beam_hbm, wigner_hbm, out_hbm, sky_ref, beam_ref, wigner, mixed, turned, copies, small, large, outs
):
    half = LOCAL // 2
    first = [
        pltpu.make_async_copy(sky_hbm, sky_ref, small.at[0]),
        pltpu.make_async_copy(beam_hbm, beam_ref, small.at[1]),
    ]
    loads = [
        pltpu.make_async_copy(
            wigner_hbm.at[0, pl.ds(i * half, half)], wigner.at[pl.ds(i * half, half)], large.at[i]
        )
        for i in range(2)
    ]
    for copy in first + loads:
        copy.start()
    for copy in first:
        copy.wait()
    sky = sky_ref[0]
    for i in range(2):
        loads[i].wait()
        for k in range(i * half, (i + 1) * half):
            weighted = (sky * beam_ref[k : k + 1, :]).astype(BF)
            mixed[2 * k : 2 * k + 2, :] = jnp.dot(weighted, wigner[k], preferred_element_type=F32)
    turned[...] = mixed[...].T
    block = jnp.concatenate(
        [turned[pl.ds(row, SHARDS, stride=4), :] for row in range(4)], axis=1
    ).astype(BF)
    for i in range(REPEAT):
        copies[i] = block
    sends = [
        pltpu.make_async_copy(copies, out_hbm.at[pl.ds(i * REPEAT, REPEAT)], outs.at[i])
        for i in range(OWNERS // REPEAT)
    ]
    for copy in sends:
        copy.start()
    for copy in sends:
        copy.wait()


def bucket_kernel(slot_ref, phi_ref, psi_ref, frac_ref, g_ref, rank_ref, carry, lhs, hot):
    zero = jnp.zeros((), BF)
    one = jnp.ones((), BF)
    own_iota = iota_bf((OWNERS, LANES), 0)
    own_wide = lax.broadcasted_iota(jnp.int32, (OWNERS, LANES), 0)
    rank_iota = iota_bf((RANKS, LANES), 0)
    before = (
        lax.broadcasted_iota(jnp.int32, (LANES, 2 * LANES), 0)
        < lax.broadcasted_iota(jnp.int32, (LANES, 2 * LANES), 1)
    ).astype(F32).astype(BF)
    carry[...] = jnp.zeros_like(carry)
    g_ref[...] = jnp.zeros_like(g_ref)

    def block(step, _):
        start = pl.multiple_of(step * 8, 8)
        slots = slot_ref[pl.ds(start, 8), :]
        owners = slots >> 2
        names = owners.astype(F32)
        rows = ((slots & 3) * 32 + phi_ref[pl.ds(start, 8), :]).astype(F32)
        psis = psi_ref[pl.ds(start, 8), :].astype(F32)
        seen = carry[...]
        ranks = []
        for u in range(8):
            mask = own_iota == names[u : u + 1].astype(BF)
            count = jnp.dot(jnp.where(mask, one, zero), before, preferred_element_type=F32)
            place = count[:, :LANES] + seen
            seen = seen + count[:, LANES:]
            rank = jnp.sum(
                jnp.where(own_wide == owners[u : u + 1], place, 0.0), axis=0, keepdims=True
            )
            ranks.append(rank)
            cut = slice(u * LANES, (u + 1) * LANES)
            hot[:, cut] = jnp.where(rank_iota == rank.astype(BF), one, zero)
            along = pl.ds(pl.multiple_of((start + u) * LANES, LANES), LANES)
            items = (rows[u : u + 1], psis[u : u + 1], frac_ref[0:1, along], frac_ref[1:2, along])
            for n, item in enumerate(items):
                lhs[n * OWNERS : (n + 1) * OWNERS, cut] = jnp.where(mask, item.astype(BF), zero)
        carry[...] = seen
        rank_ref[pl.ds(start, 8), :] = jnp.concatenate(ranks, axis=0)
        g_ref[...] += lax.dot_general(lhs[...], hot[...], NT, preferred_element_type=F32)
        return 0

    lax.fori_loop(0, 16, block, 0, unroll=4)


def eval_kernel(
    visits_ref,
    coeff_hbm,
    w_hbm,
    phi_hbm,
    g_hbm,
    slot_hbm,
    rank_hbm,
    out_ref,
    narrow,
    coeff,
    w_ref,
    phi_ref,
    g_ref,
    slot_ref,
    rank_ref,
    spec,
    tile_ref,
    found,
    parts,
    whole,
):
    quarter = OWNERS * SHARDS // 4
    pieces = [
        pltpu.make_async_copy(
            coeff_hbm.at[pl.ds(i * quarter, quarter)], narrow.at[pl.ds(i * quarter, quarter)], parts.at[i]
        )
        for i in range(4)
    ]
    others = [
        pltpu.make_async_copy(source, target, whole.at[i])
        for i, (source, target) in enumerate(
            ((w_hbm, w_ref), (phi_hbm, phi_ref), (g_hbm, g_ref), (slot_hbm, slot_ref), (rank_hbm, rank_ref))
        )
    ]
    for copy in pieces + others:
        copy.start()
    zero = jnp.zeros((), BF)
    one = jnp.ones((), BF)
    lane = lax.broadcasted_iota(jnp.int32, (1, LANES), 1) // 32

    for i in range(4):
        pieces[i].wait()

        def widen(step, _):
            start = pl.multiple_of(i * quarter + step * 256, 256)
            coeff[pl.ds(start, 256), :] = narrow[pl.ds(start, 256), :].astype(F32)
            return 0

        lax.fori_loop(0, 4, widen, 0, unroll=2)

    def spectrum(step, _):
        blocks = []
        for v in range(2):
            block = coeff[pl.ds(step * 2 + v, LANES, stride=SHARDS), :]
            turned = [block] + [pltpu.roll(block, 32 * n, axis=1) for n in (1, 2, 3)]
            for row in range(4):
                part = None
                for o in range(4):
                    piece = turned[(o - row) % 4][o * 32 : (o + 1) * 32]
                    part = piece if part is None else jnp.where(lane == o, piece, part)
                blocks.append(part.astype(BF))
        block = jnp.concatenate(blocks, axis=0)
        both = lax.dot_general(w_ref[...], block, NT, preferred_element_type=F32).astype(BF)
        for v in range(2):
            cut = both[:, v * LANES : (v + 1) * LANES]
            spec[step * 2 + v] = jnp.concatenate([cut[:NPSI], cut[NPSI:]], axis=1)
        return 0

    others[0].wait()
    lax.fori_loop(0, SHARDS // 2, spectrum, 0, unroll=4)

    def tiles(s, _):
        source = spec[s]
        for pair in range(2):
            chosen = []
            for o in (2 * pair, 2 * pair + 1):
                waves, lane_row = None, None
                for j in range(4):
                    tile = jnp.maximum(visits_ref[(o * SHARDS + s) * 4 + j], 0)
                    wave = phi_ref[o * 32 + (tile & 31)]
                    row = jnp.full((1, LANES), tile >> 5, jnp.int32)
                    waves = wave if j == 0 else jnp.where(lane == j, wave, waves)
                    lane_row = row if j == 0 else jnp.where(lane == j, row, lane_row)
                chosen.append(
                    jnp.concatenate(
                        [
                            jnp.where(lane_row == row, waves[c * 32 : (c + 1) * 32], zero)
                            for c in range(2)
                            for row in range(4)
                        ],
                        axis=0,
                    )
                )
            cells = jnp.dot(source, jnp.concatenate(chosen, axis=1), preferred_element_type=F32)
            for v in range(2):
                tile_ref[(2 * pair + v) * SHARDS + s] = cells[:, v * LANES : (v + 1) * LANES].astype(BF)
        return 0

    others[1].wait()
    lax.fori_loop(0, SHARDS, tiles, 0, unroll=4)

    row_iota = iota_bf((LANES, WIDE), 0)
    pad = jnp.zeros((1, WIDE - RANKS), F32)

    def look(step, _):
        for u in range(32):
            d = step * 32 + u
            at = [
                jnp.concatenate([g_ref[pl.ds(n * OWNERS + d, 1), :], pad], axis=1)
                for n in range(ITEMS)
            ]
            row0 = at[0].astype(BF)
            row1 = (at[0] + 1.0).astype(BF)
            q0 = at[1].astype(BF)
            q1 = jnp.where(at[1] == NPSI - 1.0, 0.0, at[1] + 1.0).astype(BF)
            a0, a1 = (1.0 - at[2]).astype(BF), at[2].astype(BF)
            b0, b1 = (1.0 - at[3]).astype(BF), at[3].astype(BF)
            hot = jnp.where(row_iota == row0, a0, jnp.where(row_iota == row1, a1, zero))
            seen = jnp.dot(tile_ref[d], hot, preferred_element_type=F32)
            weight = jnp.where(row_iota == q0, b0, jnp.where(row_iota == q1, b1, zero))
            found[pl.ds(d, 1), :] = jnp.sum(seen * weight.astype(F32), axis=0, keepdims=True)
        return 0

    others[2].wait()
    lax.fori_loop(0, OWNERS // 32, look, 0)

    others[3].wait()
    others[4].wait()
    rank_iota = iota_bf((RANKS, LANES), 0)
    own_iota = iota_bf((OWNERS, LANES), 0)

    def back(step, values):
        start = pl.multiple_of(step * 8, 8)
        owners = (slot_ref[pl.ds(start, 8), :] >> 2).astype(F32)
        ranks = rank_ref[pl.ds(start, 8), :]
        result = []
        for u in range(0, 8, 2):
            hot = jnp.concatenate(
                [
                    jnp.where(rank_iota == ranks[v : v + 1].astype(BF), one, zero)
                    for v in (u, u + 1)
                ],
                axis=1,
            )
            moved = jnp.dot(values, hot, preferred_element_type=F32).astype(BF)
            for v in (u, u + 1):
                part = moved[:, (v - u) * LANES : (v - u + 1) * LANES]
                part = jnp.where(own_iota == owners[v : v + 1].astype(BF), part, zero)
                result.append(jnp.sum(part.astype(F32), axis=0, keepdims=True))
        out_ref[pl.ds(start, 8), :] = jnp.concatenate(result, axis=0)
        return values

    lax.fori_loop(0, 16, back, found[...][:, :RANKS].astype(BF), unroll=4)


def shards(sky_coeffs, beam_coeffs, wigner, visits, point_slot, phi_cell, psi_cell, fraction):
    vmem = pl.BlockSpec(memory_space=pltpu.VMEM)
    anywhere = pl.BlockSpec(memory_space=pl.ANY)
    dma = pltpu.SemaphoreType.DMA
    copies = pl.pallas_call(
        coeff_kernel,
        out_shape=jax.ShapeDtypeStruct((OWNERS, SHARDS, LANES), BF),
        in_specs=[anywhere] * 3,
        out_specs=anywhere,
        scratch_shapes=[
            pltpu.VMEM((1, 2, DEGREES), F32),
            pltpu.VMEM((LOCAL, DEGREES), F32),
            pltpu.VMEM((LOCAL, DEGREES, LANES), BF),
            pltpu.VMEM((2 * LOCAL, LANES), F32),
            pltpu.VMEM((LANES, 2 * LOCAL), F32),
            pltpu.VMEM((REPEAT, SHARDS, LANES), BF),
            dma((2,)),
            dma((2,)),
            dma((OWNERS // REPEAT,)),
        ],
        compiler_params=pltpu.CompilerParams(vmem_limit_bytes=60 * MIB),
        cost_estimate=pl.CostEstimate(
            flops=16 * MIB, bytes_accessed=9 * MIB, transcendentals=0
        ),
        name="coeffs",
    )(sky_coeffs, beam_coeffs, wigner)
    everyone = lax.all_to_all(copies, MESH_AXES, 0, 0, tiled=True)
    slots = point_slot.reshape(OWNERS, LANES)
    grouped, ranks = pl.pallas_call(
        bucket_kernel,
        out_shape=(
            jax.ShapeDtypeStruct((ITEMS * OWNERS, RANKS), F32),
            jax.ShapeDtypeStruct((OWNERS, LANES), F32),
        ),
        in_specs=[vmem] * 4,
        out_specs=(vmem, vmem),
        scratch_shapes=[
            pltpu.VMEM((OWNERS, LANES), F32),
            pltpu.VMEM((ITEMS * OWNERS, 8 * LANES), BF),
            pltpu.VMEM((RANKS, 8 * LANES), BF),
        ],
        compiler_params=pltpu.CompilerParams(vmem_limit_bytes=24 * MIB),
        cost_estimate=pl.CostEstimate(
            flops=8 * 1024 * MIB, bytes_accessed=2 * MIB, transcendentals=0
        ),
        name="bucket",
    )(slots, phi_cell.reshape(OWNERS, LANES), psi_cell.reshape(OWNERS, LANES), fraction)
    timeline = pl.pallas_call(
        eval_kernel,
        out_shape=jax.ShapeDtypeStruct((OWNERS, LANES), F32),
        in_specs=[pl.BlockSpec(memory_space=pltpu.SMEM)] + [anywhere] * 6,
        out_specs=vmem,
        scratch_shapes=[
            pltpu.VMEM((OWNERS * SHARDS, LANES), BF),
            pltpu.VMEM((OWNERS * SHARDS, LANES), F32),
            pltpu.VMEM((2 * NPSI, LANES), BF),
            pltpu.VMEM((NPHI // 32, 2 * MODES, LANES), BF),
            pltpu.VMEM((ITEMS * OWNERS, RANKS), F32),
            pltpu.VMEM((OWNERS, LANES), jnp.int32),
            pltpu.VMEM((OWNERS, LANES), F32),
            pltpu.VMEM((SHARDS, NPSI, 2 * LANES), BF),
            pltpu.VMEM((OWNERS, NPSI, LANES), BF),
            pltpu.VMEM((OWNERS, WIDE), F32),
            dma((4,)),
            dma((5,)),
        ],
        compiler_params=pltpu.CompilerParams(vmem_limit_bytes=60 * MIB),
        cost_estimate=pl.CostEstimate(
            flops=8 * 1024 * MIB, bytes_accessed=4 * MIB, transcendentals=0
        ),
        name="evaluate",
    )(
        visits.reshape(-1),
        everyone.reshape(OWNERS * SHARDS, LANES),
        jnp.asarray(psi_tables()),
        jnp.asarray(phi_tables()),
        grouped,
        slots,
        ranks,
    )
    return timeline.reshape(-1)


def solution(mesh):
    placed = (
        P("shard", None, None),
        P("order", None),
        P("shard", "order", None, None),
        P(("order", "shard"), None, None),
        P(("order", "shard")),
        P(("order", "shard")),
        P(("order", "shard")),
        P(None, ("order", "shard")),
    )
    return jax.shard_map(
        shards, mesh=mesh, in_specs=placed, out_specs=P(("order", "shard")), check_vma=False
    )
```

```python
import math

import jax
import jax.numpy as jnp
import numpy as np
from jax import lax
from jax.experimental import pallas as pl
from jax.experimental.pallas import tpu as pltpu
from jax.sharding import PartitionSpec as P

BF = jnp.bfloat16
F32 = jnp.float32
MESH_AXES = ("order", "shard")
NPHI = 4096
NPSI = 128
MODES = 32
ORDERS = 64
GROUPS = 4
SHARDS = 32
OWNERS = 128
LANES = 128
RANKS = 192
WIDE = 256
ITEMS = 4
LOCAL = 16
DEGREES = 2048
REPEAT = 16
CHIPS = 64
PEERS = [[core + 2 * chip for chip in range(CHIPS)] for core in range(2)]
MIB = 1024 * 1024
UNROLL = 2
NT = (((1,), (1,)), ((), ()))


def phi_tables():
    phi = np.arange(NPHI, dtype=np.int64)[:, None]
    mode = np.arange(MODES, dtype=np.int64)[None, :]
    phase = ((phi * mode) % NPHI).astype(np.float64) * (2.0 * math.pi / NPHI)
    both = np.concatenate([np.cos(phase), -np.sin(phase)], axis=1)
    both = both.reshape(NPHI, 2, MODES // 2, 2).transpose(0, 1, 3, 2)
    blocks = both.reshape(NPHI // 32, 32, 2 * MODES).transpose(0, 2, 1)
    return np.tile(blocks, (1, 1, 4)).astype(jnp.bfloat16)


def psi_tables():
    psi = np.arange(NPSI, dtype=np.int64)[:, None]
    order = np.arange(ORDERS, dtype=np.int64)[None, :]
    phase = ((psi * order) % NPSI).astype(np.float64) * (2.0 * math.pi / NPSI)
    cos, sin = np.cos(phase), np.sin(phase)
    real = np.stack([cos, -sin], axis=2).reshape(NPSI, 2 * ORDERS)
    imag = np.stack([sin, cos], axis=2).reshape(NPSI, 2 * ORDERS)
    return np.concatenate([real, imag], axis=0).astype(jnp.bfloat16)


def iota_bf(shape, dim):
    return lax.broadcasted_iota(jnp.int32, shape, dim).astype(F32).astype(BF)


def coeff_kernel(
    sky_hbm, beam_hbm, wigner_hbm, out_hbm, sky_ref, beam_ref, wigner, mixed, turned, copies, small, large, outs
):
    half = LOCAL // 2
    first = [
        pltpu.make_async_copy(sky_hbm, sky_ref, small.at[0]),
        pltpu.make_async_copy(beam_hbm, beam_ref, small.at[1]),
    ]
    loads = [
        pltpu.make_async_copy(
            wigner_hbm.at[0, pl.ds(i * half, half)], wigner.at[pl.ds(i * half, half)], large.at[i]
        )
        for i in range(2)
    ]
    for copy in first + loads:
        copy.start()
    for copy in first:
        copy.wait()
    sky = sky_ref[0]
    for i in range(2):
        loads[i].wait()
        for k in range(i * half, (i + 1) * half):
            weighted = (sky * beam_ref[k : k + 1, :]).astype(BF)
            mixed[2 * k : 2 * k + 2, :] = jnp.dot(weighted, wigner[k], preferred_element_type=F32)
    turned[...] = mixed[...].T
    block = jnp.concatenate(
        [turned[pl.ds(row, SHARDS, stride=4), :] for row in range(4)], axis=1
    ).astype(BF)
    for i in range(REPEAT):
        copies[i] = block
    sends = [
        pltpu.make_async_copy(copies, out_hbm.at[pl.ds(i * REPEAT, REPEAT)], outs.at[i])
        for i in range(CHIPS // REPEAT)
    ]
    for copy in sends:
        copy.start()
    for copy in sends:
        copy.wait()


def bucket_kernel(slot_ref, phi_ref, psi_ref, frac_ref, g_ref, rank_ref, carry, lhs, hot):
    zero = jnp.zeros((), BF)
    one = jnp.ones((), BF)
    own_iota = iota_bf((OWNERS, LANES), 0)
    own_wide = lax.broadcasted_iota(jnp.int32, (OWNERS, LANES), 0)
    rank_iota = iota_bf((RANKS, LANES), 0)
    before = (
        lax.broadcasted_iota(jnp.int32, (LANES, 2 * LANES), 0)
        < lax.broadcasted_iota(jnp.int32, (LANES, 2 * LANES), 1)
    ).astype(F32).astype(BF)
    carry[...] = jnp.zeros_like(carry)
    g_ref[...] = jnp.zeros_like(g_ref)

    def block(step, _):
        start = pl.multiple_of(step * 8, 8)
        slots = slot_ref[pl.ds(start, 8), :]
        owners = slots >> 2
        names = owners.astype(F32)
        rows = ((slots & 3) * 32 + phi_ref[pl.ds(start, 8), :]).astype(F32)
        psis = psi_ref[pl.ds(start, 8), :].astype(F32)
        seen = carry[...]
        ranks = []
        for u in range(8):
            mask = own_iota == names[u : u + 1].astype(BF)
            count = jnp.dot(jnp.where(mask, one, zero), before, preferred_element_type=F32)
            place = count[:, :LANES] + seen
            seen = seen + count[:, LANES:]
            rank = jnp.sum(
                jnp.where(own_wide == owners[u : u + 1], place, 0.0), axis=0, keepdims=True
            )
            ranks.append(rank)
            cut = slice(u * LANES, (u + 1) * LANES)
            hot[:, cut] = jnp.where(rank_iota == rank.astype(BF), one, zero)
            along = pl.ds(pl.multiple_of((start + u) * LANES, LANES), LANES)
            items = (rows[u : u + 1], psis[u : u + 1], frac_ref[0:1, along], frac_ref[1:2, along])
            for n, item in enumerate(items):
                lhs[n * OWNERS : (n + 1) * OWNERS, cut] = jnp.where(mask, item.astype(BF), zero)
        carry[...] = seen
        rank_ref[pl.ds(start, 8), :] = jnp.concatenate(ranks, axis=0)
        g_ref[:, :RANKS] += lax.dot_general(lhs[...], hot[...], NT, preferred_element_type=F32)
        return 0

    lax.fori_loop(0, 16, block, 0, unroll=4)


def eval_kernel(
    visits_ref,
    core_ref,
    mine_ref,
    theirs_ref,
    w_ref,
    phi_ref,
    g_hbm,
    slot_ref,
    rank_ref,
    out_ref,
    coeff,
    spec,
    tile_ref,
    found,
    g_ref,
    sem,
):
    fetch = pltpu.make_async_copy(g_hbm, g_ref, sem)
    fetch.start()
    zero = jnp.zeros((), BF)
    one = jnp.ones((), BF)
    lane = lax.broadcasted_iota(jnp.int32, (1, LANES), 1) // 32

    for i, narrow in enumerate((mine_ref, theirs_ref)):
        side = core_ref[0] ^ i

        def widen(step, _):
            source = pl.multiple_of(step * 256, 256)
            place = (step // 2) * 4 + side * 2 + step % 2
            target = pl.multiple_of(place * 256, 256)
            coeff[pl.ds(target, 256), :] = narrow[pl.ds(source, 256), :].astype(F32)
            return 0

        lax.fori_loop(0, 8, widen, 0, unroll=2)

    def spectrum(pair):
        blocks = []
        for v in range(2):
            block = coeff[pl.ds(pair * 2 + v, LANES, stride=SHARDS), :]
            turned = [block] + [pltpu.roll(block, 32 * n, axis=1) for n in (1, 2, 3)]
            for row in range(4):
                part = None
                for o in range(4):
                    piece = turned[(o - row) % 4][o * 32 : (o + 1) * 32]
                    part = piece if part is None else jnp.where(lane == o, piece, part)
                blocks.append(part.astype(BF))
        block = jnp.concatenate(blocks, axis=0)
        both = lax.dot_general(w_ref[...], block, NT, preferred_element_type=F32).astype(BF)
        for v in range(2):
            cut = both[:, v * LANES : (v + 1) * LANES]
            spec[pair * 2 + v] = jnp.concatenate([cut[:NPSI], cut[NPSI:]], axis=1)

    def tiles(s):
        source = spec[s]
        for pair in range(2):
            chosen = []
            for o in (2 * pair, 2 * pair + 1):
                waves, lane_row = None, None
                for j in range(4):
                    tile = jnp.maximum(visits_ref[j, o * SHARDS + s], 0)
                    wave = phi_ref[o * 32 + (tile & 31)]
                    row = jnp.full((1, LANES), tile >> 5, jnp.int32)
                    waves = wave if j == 0 else jnp.where(lane == j, wave, waves)
                    lane_row = row if j == 0 else jnp.where(lane == j, row, lane_row)
                chosen.append(
                    jnp.concatenate(
                        [
                            jnp.where(lane_row == row, waves[c * 32 : (c + 1) * 32], zero)
                            for c in range(2)
                            for row in range(4)
                        ],
                        axis=0,
                    )
                )
            cells = jnp.dot(source, jnp.concatenate(chosen, axis=1), preferred_element_type=F32)
            for v in range(2):
                tile_ref[s * 4 + 2 * pair + v] = cells[:, v * LANES : (v + 1) * LANES].astype(BF)

    row_iota = iota_bf((LANES, WIDE), 0)

    def look(s):
        for o in range(4):
            d = o * SHARDS + s
            at = [g_ref[pl.ds(n * OWNERS + d, 1), :] for n in range(ITEMS)]
            row0 = at[0].astype(BF)
            row1 = (at[0] + 1.0).astype(BF)
            q0 = at[1].astype(BF)
            q1 = jnp.where(at[1] == NPSI - 1.0, 0.0, at[1] + 1.0).astype(BF)
            a0, a1 = (1.0 - at[2]).astype(BF), at[2].astype(BF)
            b0, b1 = (1.0 - at[3]).astype(BF), at[3].astype(BF)
            hot = jnp.where(row_iota == row0, a0, jnp.where(row_iota == row1, a1, zero))
            seen = jnp.dot(tile_ref[s * 4 + o], hot, preferred_element_type=F32)
            weight = jnp.where(row_iota == q0, b0, jnp.where(row_iota == q1, b1, zero))
            found[pl.ds(d, 1), :] = jnp.sum(seen * weight.astype(F32), axis=0, keepdims=True)

    def work(pair, stages):
        if 2 in stages:
            for v in range(2):
                look((pair - 2) * 2 + v)
        if 1 in stages:
            for v in range(2):
                tiles((pair - 1) * 2 + v)
        if 0 in stages:
            spectrum(pair)

    def turn(pair, _):
        work(pair, (0, 1, 2))
        return 0

    work(0, (0,))
    work(1, (0, 1))
    fetch.wait()
    lax.fori_loop(2, SHARDS // 2, turn, 0, unroll=UNROLL)
    work(SHARDS // 2, (1, 2))
    work(SHARDS // 2 + 1, (2,))

    rank_iota = iota_bf((RANKS, LANES), 0)
    own_iota = iota_bf((OWNERS, LANES), 0)

    def back(step, values):
        start = pl.multiple_of(step * 8, 8)
        owners = (slot_ref[pl.ds(start, 8), :] >> 2).astype(F32)
        ranks = rank_ref[pl.ds(start, 8), :]
        result = []
        for u in range(0, 8, 2):
            hot = jnp.concatenate(
                [
                    jnp.where(rank_iota == ranks[v : v + 1].astype(BF), one, zero)
                    for v in (u, u + 1)
                ],
                axis=1,
            )
            moved = jnp.dot(values, hot, preferred_element_type=F32).astype(BF)
            for v in (u, u + 1):
                part = moved[:, (v - u) * LANES : (v - u + 1) * LANES]
                part = jnp.where(own_iota == owners[v : v + 1].astype(BF), part, zero)
                result.append(jnp.sum(part.astype(F32), axis=0, keepdims=True))
        out_ref[pl.ds(start, 8), :] = jnp.concatenate(result, axis=0)
        return values

    lax.fori_loop(0, 16, back, found[...][:, :RANKS].astype(BF), unroll=4)


def shards(sky_coeffs, beam_coeffs, wigner, visits, point_slot, phi_cell, psi_cell, fraction):
    vmem = pl.BlockSpec(memory_space=pltpu.VMEM)
    anywhere = pl.BlockSpec(memory_space=pl.ANY)
    dma = pltpu.SemaphoreType.DMA
    copies = pl.pallas_call(
        coeff_kernel,
        out_shape=jax.ShapeDtypeStruct((CHIPS, SHARDS, LANES), BF),
        in_specs=[anywhere] * 3,
        out_specs=anywhere,
        scratch_shapes=[
            pltpu.VMEM((1, 2, DEGREES), F32),
            pltpu.VMEM((LOCAL, DEGREES), F32),
            pltpu.VMEM((LOCAL, DEGREES, LANES), BF),
            pltpu.VMEM((2 * LOCAL, LANES), F32),
            pltpu.VMEM((LANES, 2 * LOCAL), F32),
            pltpu.VMEM((REPEAT, SHARDS, LANES), BF),
            dma((2,)),
            dma((2,)),
            dma((CHIPS // REPEAT,)),
        ],
        compiler_params=pltpu.CompilerParams(vmem_limit_bytes=60 * MIB),
        cost_estimate=pl.CostEstimate(
            flops=16 * MIB, bytes_accessed=9 * MIB, transcendentals=0
        ),
        name="coeffs",
    )(sky_coeffs, beam_coeffs, wigner)
    mine = lax.all_to_all(copies, MESH_AXES, 0, 0, axis_index_groups=PEERS, tiled=True)
    core = jnp.full((1,), lax.axis_index("shard") & 1, jnp.int32)
    slots = point_slot.reshape(OWNERS, LANES)
    grouped, ranks = pl.pallas_call(
        bucket_kernel,
        out_shape=(
            jax.ShapeDtypeStruct((ITEMS * OWNERS, WIDE), F32),
            jax.ShapeDtypeStruct((OWNERS, LANES), F32),
        ),
        in_specs=[vmem] * 4,
        out_specs=(vmem, vmem),
        scratch_shapes=[
            pltpu.VMEM((OWNERS, LANES), F32),
            pltpu.VMEM((ITEMS * OWNERS, 8 * LANES), BF),
            pltpu.VMEM((RANKS, 8 * LANES), BF),
        ],
        compiler_params=pltpu.CompilerParams(vmem_limit_bytes=12 * MIB),
        cost_estimate=pl.CostEstimate(
            flops=8 * 1024 * MIB, bytes_accessed=2 * MIB, transcendentals=0
        ),
        name="bucket",
    )(slots, phi_cell.reshape(OWNERS, LANES), psi_cell.reshape(OWNERS, LANES), fraction)
    mine, ranks = lax.optimization_barrier((mine, ranks))
    theirs = lax.ppermute(mine, "shard", [(n, n ^ 1) for n in range(SHARDS)])
    timeline = pl.pallas_call(
        eval_kernel,
        out_shape=jax.ShapeDtypeStruct((OWNERS, LANES), F32),
        in_specs=[pl.BlockSpec(memory_space=pltpu.SMEM)] * 2 + [vmem] * 4 + [anywhere] + [vmem] * 2,
        out_specs=vmem,
        scratch_shapes=[
            pltpu.VMEM((OWNERS * SHARDS, LANES), F32),
            pltpu.VMEM((SHARDS, NPSI, 2 * LANES), BF),
            pltpu.VMEM((OWNERS, NPSI, LANES), BF),
            pltpu.VMEM((OWNERS, WIDE), F32),
            pltpu.VMEM((ITEMS * OWNERS, WIDE), F32),
            dma,
        ],
        compiler_params=pltpu.CompilerParams(vmem_limit_bytes=24 * MIB),
        cost_estimate=pl.CostEstimate(
            flops=8 * 1024 * MIB, bytes_accessed=4 * MIB, transcendentals=0
        ),
        name="evaluate",
    )(
        visits[0].T,
        core,
        mine.reshape(CHIPS * SHARDS, LANES),
        theirs.reshape(CHIPS * SHARDS, LANES),
        jnp.asarray(psi_tables()),
        jnp.asarray(phi_tables()),
        grouped,
        slots,
        ranks,
    )
    return timeline.reshape(-1)


def solution(mesh):
    placed = (
        P("shard", None, None),
        P("order", None),
        P("shard", "order", None, None),
        P(("order", "shard"), None, None),
        P(("order", "shard")),
        P(("order", "shard")),
        P(("order", "shard")),
        P(None, ("order", "shard")),
    )
    return jax.shard_map(
        shards, mesh=mesh, in_specs=placed, out_specs=P(("order", "shard")), check_vma=False
    )
```

```python
import math

import jax
import jax.numpy as jnp
import numpy as np
from jax import lax
from jax.experimental import pallas as pl
from jax.experimental.pallas import tpu as pltpu
from jax.sharding import PartitionSpec as P

BF = jnp.bfloat16
F32 = jnp.float32
MESH_AXES = ("order", "shard")
NPHI = 4096
NPSI = 128
MODES = 32
ORDERS = 64
GROUPS = 4
SHARDS = 32
OWNERS = 128
LANES = 128
RANKS = 192
WIDE = 256
ITEMS = 4
LOCAL = 16
DEGREES = 2048
REPEAT = 16
CHIPS = 64
PEERS = [[core + 2 * chip for chip in range(CHIPS)] for core in range(2)]
MIB = 1024 * 1024
PAIRS = 64
SPARE = 32
FIELDS = 8
LOOK = 16
BACK = 4
NT = (((1,), (1,)), ((), ()))


def phi_tables():
    phi = np.arange(NPHI, dtype=np.int64)[:, None]
    mode = np.arange(MODES, dtype=np.int64)[None, :]
    phase = ((phi * mode) % NPHI).astype(np.float64) * (2.0 * math.pi / NPHI)
    both = np.concatenate([np.cos(phase), -np.sin(phase)], axis=1)
    both = both.reshape(NPHI, 2, MODES // 2, 2).transpose(0, 1, 3, 2)
    blocks = both.reshape(NPHI // 32, 32, 2 * MODES).transpose(0, 2, 1)
    tiled = np.tile(blocks, (1, 1, 4))
    return np.concatenate([tiled, np.zeros_like(tiled[:SPARE])]).astype(jnp.bfloat16)


def psi_tables():
    psi = np.arange(NPSI, dtype=np.int64)[:, None]
    order = np.arange(ORDERS, dtype=np.int64)[None, :]
    phase = ((psi * order) % NPSI).astype(np.float64) * (2.0 * math.pi / NPSI)
    cos, sin = np.cos(phase), np.sin(phase)
    real = np.stack([cos, -sin], axis=2).reshape(NPSI, 2 * ORDERS)
    imag = np.stack([sin, cos], axis=2).reshape(NPSI, 2 * ORDERS)
    return np.concatenate([real, imag], axis=0).astype(jnp.bfloat16)


def iota_bf(shape, dim):
    return lax.broadcasted_iota(jnp.int32, shape, dim).astype(F32).astype(BF)


def coeff_kernel(
    sky_hbm, beam_hbm, wigner_hbm, out_hbm, sky_ref, beam_ref, wigner, mixed, turned, copies, small, large, outs
):
    half = LOCAL // 2
    first = [
        pltpu.make_async_copy(sky_hbm, sky_ref, small.at[0]),
        pltpu.make_async_copy(beam_hbm, beam_ref, small.at[1]),
    ]
    loads = [
        pltpu.make_async_copy(
            wigner_hbm.at[0, pl.ds(i * half, half)], wigner.at[pl.ds(i * half, half)], large.at[i]
        )
        for i in range(2)
    ]
    for copy in first + loads:
        copy.start()
    for copy in first:
        copy.wait()
    sky = sky_ref[0]
    for i in range(2):
        loads[i].wait()
        for k in range(i * half, (i + 1) * half):
            weighted = (sky * beam_ref[k : k + 1, :]).astype(BF)
            mixed[2 * k : 2 * k + 2, :] = jnp.dot(weighted, wigner[k], preferred_element_type=F32)
    turned[...] = mixed[...].T
    block = jnp.concatenate(
        [turned[pl.ds(row, SHARDS, stride=4), :] for row in range(4)], axis=1
    ).astype(BF)
    for i in range(REPEAT):
        copies[i] = block
    sends = [
        pltpu.make_async_copy(copies, out_hbm.at[pl.ds(i * REPEAT, REPEAT)], outs.at[i])
        for i in range(CHIPS // REPEAT)
    ]
    for copy in sends:
        copy.start()
    for copy in sends:
        copy.wait()


def bucket_kernel(slot_ref, phi_ref, psi_ref, frac_ref, *refs):
    fields, (ids_ref, pair_ref, lane_ref, g_ref, rank_ref, carry, lhs, hot) = refs[:FIELDS], refs[FIELDS:]
    zero = jnp.zeros((), BF)
    one = jnp.ones((), BF)
    own_iota = iota_bf((OWNERS, LANES), 0)
    own_wide = lax.broadcasted_iota(jnp.int32, (OWNERS, LANES), 0)
    rank_iota = iota_bf((RANKS, LANES), 0)
    before = (
        lax.broadcasted_iota(jnp.int32, (LANES, 2 * LANES), 0)
        < lax.broadcasted_iota(jnp.int32, (LANES, 2 * LANES), 1)
    ).astype(F32).astype(BF)
    carry[...] = jnp.zeros_like(carry)
    g_ref[...] = jnp.zeros_like(g_ref)

    def block(step, _):
        start = pl.multiple_of(step * 8, 8)
        slots = slot_ref[pl.ds(start, 8), :]
        owners = slots >> 2
        names = owners.astype(F32)
        rows = ((slots & 3) * 32 + phi_ref[pl.ds(start, 8), :]).astype(F32)
        psis = psi_ref[pl.ds(start, 8), :].astype(F32)
        seen = carry[...]
        ranks = []
        for u in range(8):
            mask = own_iota == names[u : u + 1].astype(BF)
            count = jnp.dot(jnp.where(mask, one, zero), before, preferred_element_type=F32)
            place = count[:, :LANES] + seen
            seen = seen + count[:, LANES:]
            rank = jnp.sum(
                jnp.where(own_wide == owners[u : u + 1], place, 0.0), axis=0, keepdims=True
            )
            ranks.append(rank)
            cut = slice(u * LANES, (u + 1) * LANES)
            hot[:, cut] = jnp.where(rank_iota == rank.astype(BF), one, zero)
            along = pl.ds(pl.multiple_of((start + u) * LANES, LANES), LANES)
            items = (rows[u : u + 1], psis[u : u + 1], frac_ref[0:1, along], frac_ref[1:2, along])
            for n, item in enumerate(items):
                lhs[n * OWNERS : (n + 1) * OWNERS, cut] = jnp.where(mask, item.astype(BF), zero)
        carry[...] = seen
        rank_ref[pl.ds(start, 8), :] = jnp.concatenate(ranks, axis=0)
        g_ref[:, :RANKS] += lax.dot_general(lhs[...], hot[...], NT, preferred_element_type=F32)
        return 0

    lax.fori_loop(0, 16, block, 0, unroll=4)

    square = (OWNERS, OWNERS)
    across = lax.broadcasted_iota(jnp.int32, square, 1).astype(F32)
    down = lax.broadcasted_iota(jnp.int32, square, 0).astype(F32)
    heavy = carry[...] > 128.0
    earlier = jnp.where(across < down, 1.0, 0.0).astype(BF)
    ahead = jnp.dot(
        earlier, jnp.where(heavy, 1.0, 0.0).astype(BF), preferred_element_type=F32
    )
    pair = jnp.where(heavy, ahead, down - ahead)
    here = pair == across
    first = jnp.where(heavy, jnp.where(here, 1.0, 0.0), 0.0)
    second = jnp.where(heavy, 0.0, jnp.where(here, 1.0, 0.0))
    ids_ref[...] = jnp.concatenate(
        [jnp.sum(pick * down, axis=0, keepdims=True) for pick in (first, second)], axis=0
    ).astype(jnp.int32)
    first = first.T[:PAIRS].astype(BF)
    second = second.T[:PAIRS].astype(BF)
    late = lax.broadcasted_iota(jnp.int32, (PAIRS, WIDE), 1) >= RANKS
    merged = []
    for n in range(ITEMS):
        values = g_ref[n * OWNERS : (n + 1) * OWNERS, :].astype(BF)
        long = jnp.dot(first, values, preferred_element_type=F32)
        short = jnp.dot(second, values, preferred_element_type=F32)
        merged.append(jnp.where(late, pltpu.roll(short, RANKS, axis=1), long))
    row, psi, a, b = merged
    row = jnp.where(late, row + 128.0, row)
    fields[0][...] = row
    fields[1][...] = row + 1.0
    fields[2][...] = psi
    fields[3][...] = jnp.where(psi == NPSI - 1.0, 0.0, psi + 1.0)
    fields[4][...] = 1.0 - a
    fields[5][...] = a
    fields[6][...] = 1.0 - b
    fields[7][...] = b
    lane_ref[...] = jnp.where(heavy, pair, pair + 64.0)

    def address(step, code):
        start = pl.multiple_of(step * 8, 8)
        owners = slot_ref[pl.ds(start, 8), :] >> 2
        found = jnp.concatenate(
            [
                jnp.sum(
                    jnp.where(own_wide == owners[u : u + 1], code[...], 0.0), axis=0, keepdims=True
                )
                for u in range(8)
            ],
            axis=0,
        )
        light = found >= 64.0
        pair_ref[pl.ds(start, 8), :] = jnp.where(light, found - 64.0, found)
        rank_ref[pl.ds(start, 8), :] += jnp.where(light, 1.0 * RANKS, 0.0)
        return code

    carry[...] = lane_ref[...]
    lax.fori_loop(0, 16, lambda step, _: (address(step, carry), 0)[1], 0, unroll=2)
    lane_ref[...] = rank_ref[...]


def eval_kernel(
    visits_ref,
    core_ref,
    ids_ref,
    mine_ref,
    theirs_ref,
    w_ref,
    phi_ref,
    pair_ref,
    lane_ref,
    *refs,
):
    fields, (out_ref, coeff, spec, tile_ref, found) = refs[:FIELDS], refs[FIELDS:]
    zero = jnp.zeros((), BF)
    one = jnp.ones((), BF)
    lane = lax.broadcasted_iota(jnp.int32, (1, LANES), 1) // 32

    for i, narrow in enumerate((mine_ref, theirs_ref)):
        side = core_ref[0] ^ i

        def widen(step, _):
            source = pl.multiple_of(step * 256, 256)
            place = (step // 2) * 4 + side * 2 + step % 2
            target = pl.multiple_of(place * 256, 256)
            coeff[pl.ds(target, 256), :] = narrow[pl.ds(source, 256), :].astype(F32)
            return 0

        lax.fori_loop(0, 8, widen, 0, unroll=2)

    def spectrum(pair):
        blocks = []
        for v in range(2):
            block = coeff[pl.ds(pair * 2 + v, LANES, stride=SHARDS), :]
            turned = [block] + [pltpu.roll(block, 32 * n, axis=1) for n in (1, 2, 3)]
            for row in range(4):
                part = None
                for o in range(4):
                    piece = turned[(o - row) % 4][o * 32 : (o + 1) * 32]
                    part = piece if part is None else jnp.where(lane == o, piece, part)
                blocks.append(part.astype(BF))
        block = jnp.concatenate(blocks, axis=0)
        both = lax.dot_general(w_ref[...], block, NT, preferred_element_type=F32).astype(BF)
        for v in range(2):
            cut = both[:, v * LANES : (v + 1) * LANES]
            spec[pair * 2 + v] = jnp.concatenate([cut[:NPSI], cut[NPSI:]], axis=1)

    def tiles(s):
        source = spec[s]
        for pair in range(2):
            chosen = []
            for o in (2 * pair, 2 * pair + 1):
                waves, lane_row = None, None
                for j in range(4):
                    tile = jnp.maximum(visits_ref[j, o * SHARDS + s], 0)
                    wave = phi_ref[o * 32 + (tile & 31)]
                    row = jnp.full((1, LANES), tile >> 5, jnp.int32)
                    waves = wave if j == 0 else jnp.where(lane == j, wave, waves)
                    lane_row = row if j == 0 else jnp.where(lane == j, row, lane_row)
                chosen.append(
                    jnp.concatenate(
                        [
                            jnp.where(lane_row == row, waves[c * 32 : (c + 1) * 32], zero)
                            for c in range(2)
                            for row in range(4)
                        ],
                        axis=0,
                    )
                )
            cells = jnp.dot(source, jnp.concatenate(chosen, axis=1), preferred_element_type=F32)
            for v in range(2):
                tile_ref[(2 * pair + v) * SHARDS + s] = cells[:, v * LANES : (v + 1) * LANES].astype(BF)

    def turn(pair, _):
        for v in range(2):
            tiles((pair - 1) * 2 + v)
        spectrum(pair)
        return 0

    spectrum(0)
    lax.fori_loop(1, SHARDS // 2, turn, 0, unroll=3)
    for v in range(2):
        tiles(SHARDS - 2 + v)

    near = iota_bf((LANES, WIDE), 0)
    far = near[:, LANES:] + jnp.asarray(128.0, BF)
    empty = jnp.zeros((LANES, LANES), BF)

    def look(step, _):
        for u in range(LOOK):
            p = step * LOOK + u
            row0, row1, q0, q1, a0, a1, b0, b1 = [
                field[pl.ds(p, 1), :].astype(BF) for field in fields
            ]
            top = jnp.where(near == row0, a0, jnp.where(near == row1, a1, zero))
            low = jnp.where(
                far == row0[:, LANES:],
                a0[:, LANES:],
                jnp.where(far == row1[:, LANES:], a1[:, LANES:], zero),
            )
            hot = jnp.concatenate([top, jnp.concatenate([empty, low], axis=1)], axis=0)
            both = jnp.concatenate([tile_ref[ids_ref[0, p]], tile_ref[ids_ref[1, p]]], axis=1)
            seen = jnp.dot(both, hot, preferred_element_type=F32)
            weight = jnp.where(near == q0, b0, jnp.where(near == q1, b1, zero))
            found[pl.ds(p, 1), :] = jnp.sum(seen * weight.astype(F32), axis=0, keepdims=True)
        return 0

    lax.fori_loop(0, PAIRS // LOOK, look, 0)

    lane_iota = iota_bf((WIDE, LANES), 0)
    pair_iota = iota_bf((PAIRS, LANES), 0)

    def back(step, values):
        start = pl.multiple_of(step * 8, 8)
        pairs = pair_ref[pl.ds(start, 8), :]
        lanes = lane_ref[pl.ds(start, 8), :]
        result = []
        for u in range(0, 8, 2):
            hot = jnp.concatenate(
                [
                    jnp.where(lane_iota == lanes[v : v + 1].astype(BF), one, zero)
                    for v in (u, u + 1)
                ],
                axis=1,
            )
            moved = jnp.dot(values, hot, preferred_element_type=F32).astype(BF)
            for v in (u, u + 1):
                part = moved[:, (v - u) * LANES : (v - u + 1) * LANES]
                part = jnp.where(pair_iota == pairs[v : v + 1].astype(BF), part, zero)
                part = part[:32] + part[32:]
                part = (part[:16] + part[16:]).astype(F32)
                result.append(jnp.sum(part, axis=0, keepdims=True))
        out_ref[pl.ds(start, 8), :] = jnp.concatenate(result, axis=0)
        return values

    lax.fori_loop(0, 16, back, found[...].astype(BF), unroll=BACK)


def shards(sky_coeffs, beam_coeffs, wigner, visits, point_slot, phi_cell, psi_cell, fraction):
    vmem = pl.BlockSpec(memory_space=pltpu.VMEM)
    anywhere = pl.BlockSpec(memory_space=pl.ANY)
    dma = pltpu.SemaphoreType.DMA
    copies = pl.pallas_call(
        coeff_kernel,
        out_shape=jax.ShapeDtypeStruct((CHIPS, SHARDS, LANES), BF),
        in_specs=[anywhere] * 3,
        out_specs=anywhere,
        scratch_shapes=[
            pltpu.VMEM((1, 2, DEGREES), F32),
            pltpu.VMEM((LOCAL, DEGREES), F32),
            pltpu.VMEM((LOCAL, DEGREES, LANES), BF),
            pltpu.VMEM((2 * LOCAL, LANES), F32),
            pltpu.VMEM((LANES, 2 * LOCAL), F32),
            pltpu.VMEM((REPEAT, SHARDS, LANES), BF),
            dma((2,)),
            dma((2,)),
            dma((CHIPS // REPEAT,)),
        ],
        compiler_params=pltpu.CompilerParams(vmem_limit_bytes=60 * MIB),
        cost_estimate=pl.CostEstimate(
            flops=16 * MIB, bytes_accessed=9 * MIB, transcendentals=0
        ),
        name="coeffs",
    )(sky_coeffs, beam_coeffs, wigner)
    mine = lax.all_to_all(copies, MESH_AXES, 0, 0, axis_index_groups=PEERS, tiled=True)
    core = jnp.full((1,), lax.axis_index("shard") & 1, jnp.int32)
    slots = point_slot.reshape(OWNERS, LANES)
    table = jax.ShapeDtypeStruct((OWNERS, LANES), F32)
    *fields, ids, pairs, lanes = pl.pallas_call(
        bucket_kernel,
        out_shape=[jax.ShapeDtypeStruct((PAIRS, WIDE), F32)] * FIELDS
        + [jax.ShapeDtypeStruct((2, OWNERS), jnp.int32), table, table],
        in_specs=[vmem] * 4,
        out_specs=[vmem] * (FIELDS + 3),
        scratch_shapes=[
            pltpu.VMEM((ITEMS * OWNERS, WIDE), F32),
            pltpu.VMEM((OWNERS, LANES), F32),
            pltpu.VMEM((OWNERS, LANES), F32),
            pltpu.VMEM((ITEMS * OWNERS, 8 * LANES), BF),
            pltpu.VMEM((RANKS, 8 * LANES), BF),
        ],
        compiler_params=pltpu.CompilerParams(vmem_limit_bytes=12 * MIB),
        cost_estimate=pl.CostEstimate(
            flops=8 * 1024 * MIB, bytes_accessed=2 * MIB, transcendentals=0
        ),
        name="bucket",
    )(slots, phi_cell.reshape(OWNERS, LANES), psi_cell.reshape(OWNERS, LANES), fraction)
    mine, lanes = lax.optimization_barrier((mine, lanes))
    theirs = lax.ppermute(mine, "shard", [(n, n ^ 1) for n in range(SHARDS)])
    timeline = pl.pallas_call(
        eval_kernel,
        out_shape=jax.ShapeDtypeStruct((OWNERS, LANES), F32),
        in_specs=[pl.BlockSpec(memory_space=pltpu.SMEM)] * 3 + [vmem] * (6 + FIELDS),
        out_specs=vmem,
        scratch_shapes=[
            pltpu.VMEM((OWNERS * SHARDS, LANES), F32),
            pltpu.VMEM((SHARDS, NPSI, 2 * LANES), BF),
            pltpu.VMEM((OWNERS, NPSI, LANES), BF),
            pltpu.VMEM((PAIRS, WIDE), F32),
        ],
        compiler_params=pltpu.CompilerParams(vmem_limit_bytes=24 * MIB),
        cost_estimate=pl.CostEstimate(
            flops=8 * 1024 * MIB, bytes_accessed=4 * MIB, transcendentals=0
        ),
        name="evaluate",
    )(
        visits[0].T,
        core,
        ids,
        mine.reshape(CHIPS * SHARDS, LANES),
        theirs.reshape(CHIPS * SHARDS, LANES),
        jnp.asarray(psi_tables()),
        jnp.asarray(phi_tables()),
        pairs,
        lanes,
        *fields,
    )
    return timeline.reshape(-1)


def solution(mesh):
    placed = (
        P("shard", None, None),
        P("order", None),
        P("shard", "order", None, None),
        P(("order", "shard"), None, None),
        P(("order", "shard")),
        P(("order", "shard")),
        P(("order", "shard")),
        P(None, ("order", "shard")),
    )
    return jax.shard_map(
        shards, mesh=mesh, in_specs=placed, out_specs=P(("order", "shard")), check_vma=False
    )
```

```python
import math

import jax
import jax.numpy as jnp
import numpy as np
from jax import lax
from jax.experimental import pallas as pl
from jax.experimental.pallas import tpu as pltpu
from jax.sharding import PartitionSpec as P

BF = jnp.bfloat16
F32 = jnp.float32
MESH_AXES = ("order", "shard")
NPHI = 4096
NPSI = 128
MODES = 32
ORDERS = 64
GROUPS = 4
SHARDS = 32
OWNERS = 128
LANES = 128
RANKS = 192
WIDE = 256
ITEMS = 4
LOCAL = 16
DEGREES = 2048
REPEAT = 16
CHIPS = 64
PEERS = [[core + 2 * chip for chip in range(CHIPS)] for core in range(2)]
MIB = 1024 * 1024
PAIRS = 64
FIELDS = 8
LOOK = 16
BACK = 4
NT = (((1,), (1,)), ((), ()))


def phi_tables():
    phi = np.arange(NPHI, dtype=np.int64)[:, None]
    mode = np.arange(MODES, dtype=np.int64)[None, :]
    phase = ((phi * mode) % NPHI).astype(np.float64) * (2.0 * math.pi / NPHI)
    both = np.concatenate([np.cos(phase), -np.sin(phase)], axis=1)
    both = both.reshape(NPHI, 2, MODES // 2, 2).transpose(0, 1, 3, 2)
    blocks = both.reshape(NPHI // LANES, LANES, 2 * MODES).transpose(0, 2, 1)
    return blocks.astype(jnp.bfloat16)


def psi_tables():
    psi = np.arange(NPSI, dtype=np.int64)[:, None]
    order = np.arange(ORDERS, dtype=np.int64)[None, :]
    phase = ((psi * order) % NPSI).astype(np.float64) * (2.0 * math.pi / NPSI)
    cos, sin = np.cos(phase), np.sin(phase)
    real = np.stack([cos, -sin], axis=2).reshape(NPSI, 2 * ORDERS)
    imag = np.stack([sin, cos], axis=2).reshape(NPSI, 2 * ORDERS)
    return np.concatenate([real, imag], axis=0).astype(jnp.bfloat16)


def iota_bf(shape, dim):
    return lax.broadcasted_iota(jnp.int32, shape, dim).astype(F32).astype(BF)


def coeff_kernel(
    sky_hbm, beam_hbm, wigner_hbm, out_hbm, sky_ref, beam_ref, wigner, mixed, turned, copies, small, large, outs
):
    half = LOCAL // 2
    first = [
        pltpu.make_async_copy(sky_hbm, sky_ref, small.at[0]),
        pltpu.make_async_copy(beam_hbm, beam_ref, small.at[1]),
    ]
    loads = [
        pltpu.make_async_copy(
            wigner_hbm.at[0, pl.ds(i * half, half)], wigner.at[pl.ds(i * half, half)], large.at[i]
        )
        for i in range(2)
    ]
    for copy in first + loads:
        copy.start()
    for copy in first:
        copy.wait()
    sky = sky_ref[0]
    for i in range(2):
        loads[i].wait()
        for k in range(i * half, (i + 1) * half):
            weighted = (sky * beam_ref[k : k + 1, :]).astype(BF)
            mixed[2 * k : 2 * k + 2, :] = jnp.dot(weighted, wigner[k], preferred_element_type=F32)
    turned[...] = mixed[...].T
    block = jnp.concatenate(
        [turned[pl.ds(row, SHARDS, stride=4), :] for row in range(4)], axis=1
    ).astype(BF)
    for i in range(REPEAT):
        copies[i] = block
    sends = [
        pltpu.make_async_copy(copies, out_hbm.at[pl.ds(i * REPEAT, REPEAT)], outs.at[i])
        for i in range(CHIPS // REPEAT)
    ]
    for copy in sends:
        copy.start()
    for copy in sends:
        copy.wait()


def bucket_kernel(slot_ref, phi_ref, psi_ref, frac_ref, *refs):
    fields, (ids_ref, pair_ref, lane_ref, g_ref, rank_ref, carry, lhs, hot) = refs[:FIELDS], refs[FIELDS:]
    zero = jnp.zeros((), BF)
    one = jnp.ones((), BF)
    own_iota = iota_bf((OWNERS, LANES), 0)
    own_wide = lax.broadcasted_iota(jnp.int32, (OWNERS, LANES), 0)
    rank_iota = iota_bf((RANKS, LANES), 0)
    before = (
        lax.broadcasted_iota(jnp.int32, (LANES, 2 * LANES), 0)
        < lax.broadcasted_iota(jnp.int32, (LANES, 2 * LANES), 1)
    ).astype(F32).astype(BF)
    carry[...] = jnp.zeros_like(carry)
    g_ref[...] = jnp.zeros_like(g_ref)

    def block(step, _):
        start = pl.multiple_of(step * 8, 8)
        slots = slot_ref[pl.ds(start, 8), :]
        owners = slots >> 2
        names = owners.astype(F32)
        rows = ((slots & 3) * 32 + phi_ref[pl.ds(start, 8), :]).astype(F32)
        psis = psi_ref[pl.ds(start, 8), :].astype(F32)
        seen = carry[...]
        ranks = []
        for u in range(8):
            mask = own_iota == names[u : u + 1].astype(BF)
            count = jnp.dot(jnp.where(mask, one, zero), before, preferred_element_type=F32)
            place = count[:, :LANES] + seen
            seen = seen + count[:, LANES:]
            rank = jnp.sum(
                jnp.where(own_wide == owners[u : u + 1], place, 0.0), axis=0, keepdims=True
            )
            ranks.append(rank)
            cut = slice(u * LANES, (u + 1) * LANES)
            hot[:, cut] = jnp.where(rank_iota == rank.astype(BF), one, zero)
            along = pl.ds(pl.multiple_of((start + u) * LANES, LANES), LANES)
            items = (rows[u : u + 1], psis[u : u + 1], frac_ref[0:1, along], frac_ref[1:2, along])
            for n, item in enumerate(items):
                lhs[n * OWNERS : (n + 1) * OWNERS, cut] = jnp.where(mask, item.astype(BF), zero)
        carry[...] = seen
        rank_ref[pl.ds(start, 8), :] = jnp.concatenate(ranks, axis=0)
        g_ref[:, :RANKS] += lax.dot_general(lhs[...], hot[...], NT, preferred_element_type=F32)
        return 0

    lax.fori_loop(0, 16, block, 0, unroll=4)

    square = (OWNERS, OWNERS)
    across = lax.broadcasted_iota(jnp.int32, square, 1).astype(F32)
    down = lax.broadcasted_iota(jnp.int32, square, 0).astype(F32)
    heavy = carry[...] > 128.0
    earlier = jnp.where(across < down, 1.0, 0.0).astype(BF)
    ahead = jnp.dot(
        earlier, jnp.where(heavy, 1.0, 0.0).astype(BF), preferred_element_type=F32
    )
    pair = jnp.where(heavy, ahead, down - ahead)
    here = pair == across
    first = jnp.where(heavy, jnp.where(here, 1.0, 0.0), 0.0)
    second = jnp.where(heavy, 0.0, jnp.where(here, 1.0, 0.0))
    ids_ref[...] = jnp.concatenate(
        [jnp.sum(pick * down, axis=0, keepdims=True) for pick in (first, second)], axis=0
    ).astype(jnp.int32)
    first = first.T[:PAIRS].astype(BF)
    second = second.T[:PAIRS].astype(BF)
    late = lax.broadcasted_iota(jnp.int32, (PAIRS, WIDE), 1) >= RANKS
    merged = []
    for n in range(ITEMS):
        values = g_ref[n * OWNERS : (n + 1) * OWNERS, :].astype(BF)
        long = jnp.dot(first, values, preferred_element_type=F32)
        short = jnp.dot(second, values, preferred_element_type=F32)
        merged.append(jnp.where(late, pltpu.roll(short, RANKS, axis=1), long))
    row, psi, a, b = merged
    row = jnp.where(late, row + 128.0, row)
    fields[0][...] = row
    fields[1][...] = row + 1.0
    fields[2][...] = psi
    fields[3][...] = jnp.where(psi == NPSI - 1.0, 0.0, psi + 1.0)
    fields[4][...] = 1.0 - a
    fields[5][...] = a
    fields[6][...] = 1.0 - b
    fields[7][...] = b
    lane_ref[...] = jnp.where(heavy, pair, pair + 64.0)

    def address(step, code):
        start = pl.multiple_of(step * 8, 8)
        owners = slot_ref[pl.ds(start, 8), :] >> 2
        found = jnp.concatenate(
            [
                jnp.sum(
                    jnp.where(own_wide == owners[u : u + 1], code[...], 0.0), axis=0, keepdims=True
                )
                for u in range(8)
            ],
            axis=0,
        )
        light = found >= 64.0
        pair_ref[pl.ds(start, 8), :] = jnp.where(light, found - 64.0, found)
        rank_ref[pl.ds(start, 8), :] += jnp.where(light, 1.0 * RANKS, 0.0)
        return code

    carry[...] = lane_ref[...]
    lax.fori_loop(0, 16, lambda step, _: (address(step, carry), 0)[1], 0, unroll=2)
    lane_ref[...] = rank_ref[...]


def eval_kernel(
    visits_ref,
    core_ref,
    ids_ref,
    mine_ref,
    theirs_ref,
    w_ref,
    phi_ref,
    pair_ref,
    lane_ref,
    *refs,
):
    fields, (out_ref, coeff, spec, tile_ref, found) = refs[:FIELDS], refs[FIELDS:]
    zero = jnp.zeros((), BF)
    one = jnp.ones((), BF)
    lane = lax.broadcasted_iota(jnp.int32, (1, LANES), 1) // 32

    for i, narrow in enumerate((mine_ref, theirs_ref)):
        side = core_ref[0] ^ i

        def widen(step, _):
            source = pl.multiple_of(step * 256, 256)
            place = (step // 2) * 4 + side * 2 + step % 2
            target = pl.multiple_of(place * 256, 256)
            coeff[pl.ds(target, 256), :] = narrow[pl.ds(source, 256), :].astype(F32)
            return 0

        lax.fori_loop(0, 8, widen, 0, unroll=2)

    def spectrum(pair):
        blocks = []
        for v in range(2):
            block = coeff[pl.ds(pair * 2 + v, LANES, stride=SHARDS), :]
            turned = [block] + [pltpu.roll(block, 32 * n, axis=1) for n in (1, 2, 3)]
            for row in range(4):
                part = None
                for o in range(4):
                    piece = turned[(o - row) % 4][o * 32 : (o + 1) * 32]
                    part = piece if part is None else jnp.where(lane == o, piece, part)
                blocks.append(part.astype(BF))
        block = jnp.concatenate(blocks, axis=0)
        both = lax.dot_general(w_ref[...], block, NT, preferred_element_type=F32).astype(BF)
        for v in range(2):
            cut = both[:, v * LANES : (v + 1) * LANES]
            spec[pair * 2 + v] = jnp.concatenate([cut[:NPSI], cut[NPSI:]], axis=1)

    def tiles(s):
        source = spec[s]
        for pair in range(2):
            chosen = []
            for o in (2 * pair, 2 * pair + 1):
                waves, lane_row = None, None
                for j in range(4):
                    tile = jnp.maximum(visits_ref[j, o * SHARDS + s], 0)
                    turn_by = ((j - tile) & 3) * 32
                    wave = pltpu.roll(phi_ref[o * 8 + ((tile & 31) >> 2)], turn_by, axis=1)
                    row = jnp.full((1, LANES), tile >> 5, jnp.int32)
                    waves = wave if j == 0 else jnp.where(lane == j, wave, waves)
                    lane_row = row if j == 0 else jnp.where(lane == j, row, lane_row)
                chosen.append(
                    jnp.concatenate(
                        [
                            jnp.where(lane_row == row, waves[c * 32 : (c + 1) * 32], zero)
                            for c in range(2)
                            for row in range(4)
                        ],
                        axis=0,
                    )
                )
            cells = jnp.dot(source, jnp.concatenate(chosen, axis=1), preferred_element_type=F32)
            for v in range(2):
                tile_ref[(2 * pair + v) * SHARDS + s] = cells[:, v * LANES : (v + 1) * LANES].astype(BF)

    def turn(pair, _):
        for v in range(2):
            tiles((pair - 1) * 2 + v)
        spectrum(pair)
        return 0

    spectrum(0)
    lax.fori_loop(1, SHARDS // 2, turn, 0, unroll=3)
    for v in range(2):
        tiles(SHARDS - 2 + v)

    near = iota_bf((LANES, WIDE), 0)
    far = near[:, LANES:] + jnp.asarray(128.0, BF)
    empty = jnp.zeros((LANES, LANES), BF)

    def look(step, _):
        for u in range(LOOK):
            p = step * LOOK + u
            row0, row1, q0, q1, a0, a1, b0, b1 = [
                field[pl.ds(p, 1), :].astype(BF) for field in fields
            ]
            top = jnp.where(near == row0, a0, jnp.where(near == row1, a1, zero))
            low = jnp.where(
                far == row0[:, LANES:],
                a0[:, LANES:],
                jnp.where(far == row1[:, LANES:], a1[:, LANES:], zero),
            )
            hot = jnp.concatenate([top, jnp.concatenate([empty, low], axis=1)], axis=0)
            both = jnp.concatenate([tile_ref[ids_ref[0, p]], tile_ref[ids_ref[1, p]]], axis=1)
            seen = jnp.dot(both, hot, preferred_element_type=F32)
            weight = jnp.where(near == q0, b0, jnp.where(near == q1, b1, zero))
            found[pl.ds(p, 1), :] = jnp.sum(seen * weight.astype(F32), axis=0, keepdims=True)
        return 0

    lax.fori_loop(0, PAIRS // LOOK, look, 0)

    lane_iota = iota_bf((WIDE, LANES), 0)
    pair_iota = iota_bf((PAIRS, LANES), 0)

    def back(step, values):
        start = pl.multiple_of(step * 8, 8)
        pairs = pair_ref[pl.ds(start, 8), :]
        lanes = lane_ref[pl.ds(start, 8), :]
        result = []
        for u in range(0, 8, 2):
            hot = jnp.concatenate(
                [
                    jnp.where(lane_iota == lanes[v : v + 1].astype(BF), one, zero)
                    for v in (u, u + 1)
                ],
                axis=1,
            )
            moved = jnp.dot(values, hot, preferred_element_type=F32).astype(BF)
            for v in (u, u + 1):
                part = moved[:, (v - u) * LANES : (v - u + 1) * LANES]
                part = jnp.where(pair_iota == pairs[v : v + 1].astype(BF), part, zero)
                part = part[:32] + part[32:]
                part = (part[:16] + part[16:]).astype(F32)
                result.append(jnp.sum(part, axis=0, keepdims=True))
        out_ref[pl.ds(start, 8), :] = jnp.concatenate(result, axis=0)
        return values

    lax.fori_loop(0, 16, back, found[...].astype(BF), unroll=BACK)


def shards(sky_coeffs, beam_coeffs, wigner, visits, point_slot, phi_cell, psi_cell, fraction):
    vmem = pl.BlockSpec(memory_space=pltpu.VMEM)
    anywhere = pl.BlockSpec(memory_space=pl.ANY)
    dma = pltpu.SemaphoreType.DMA
    copies = pl.pallas_call(
        coeff_kernel,
        out_shape=jax.ShapeDtypeStruct((CHIPS, SHARDS, LANES), BF),
        in_specs=[anywhere] * 3,
        out_specs=anywhere,
        scratch_shapes=[
            pltpu.VMEM((1, 2, DEGREES), F32),
            pltpu.VMEM((LOCAL, DEGREES), F32),
            pltpu.VMEM((LOCAL, DEGREES, LANES), BF),
            pltpu.VMEM((2 * LOCAL, LANES), F32),
            pltpu.VMEM((LANES, 2 * LOCAL), F32),
            pltpu.VMEM((REPEAT, SHARDS, LANES), BF),
            dma((2,)),
            dma((2,)),
            dma((CHIPS // REPEAT,)),
        ],
        compiler_params=pltpu.CompilerParams(vmem_limit_bytes=60 * MIB),
        cost_estimate=pl.CostEstimate(
            flops=16 * MIB, bytes_accessed=9 * MIB, transcendentals=0
        ),
        name="coeffs",
    )(sky_coeffs, beam_coeffs, wigner)
    mine = lax.all_to_all(copies, MESH_AXES, 0, 0, axis_index_groups=PEERS, tiled=True)
    core = jnp.full((1,), lax.axis_index("shard") & 1, jnp.int32)
    slots = point_slot.reshape(OWNERS, LANES)
    table = jax.ShapeDtypeStruct((OWNERS, LANES), F32)
    *fields, ids, pairs, lanes = pl.pallas_call(
        bucket_kernel,
        out_shape=[jax.ShapeDtypeStruct((PAIRS, WIDE), F32)] * FIELDS
        + [jax.ShapeDtypeStruct((2, OWNERS), jnp.int32), table, table],
        in_specs=[vmem] * 4,
        out_specs=[vmem] * (FIELDS + 3),
        scratch_shapes=[
            pltpu.VMEM((ITEMS * OWNERS, WIDE), F32),
            pltpu.VMEM((OWNERS, LANES), F32),
            pltpu.VMEM((OWNERS, LANES), F32),
            pltpu.VMEM((ITEMS * OWNERS, 8 * LANES), BF),
            pltpu.VMEM((RANKS, 8 * LANES), BF),
        ],
        compiler_params=pltpu.CompilerParams(vmem_limit_bytes=12 * MIB),
        cost_estimate=pl.CostEstimate(
            flops=8 * 1024 * MIB, bytes_accessed=2 * MIB, transcendentals=0
        ),
        name="bucket",
    )(slots, phi_cell.reshape(OWNERS, LANES), psi_cell.reshape(OWNERS, LANES), fraction)
    mine, lanes = lax.optimization_barrier((mine, lanes))
    theirs = lax.ppermute(mine, "shard", [(n, n ^ 1) for n in range(SHARDS)])
    timeline = pl.pallas_call(
        eval_kernel,
        out_shape=jax.ShapeDtypeStruct((OWNERS, LANES), F32),
        in_specs=[pl.BlockSpec(memory_space=pltpu.SMEM)] * 3 + [vmem] * (6 + FIELDS),
        out_specs=vmem,
        scratch_shapes=[
            pltpu.VMEM((OWNERS * SHARDS, LANES), F32),
            pltpu.VMEM((SHARDS, NPSI, 2 * LANES), BF),
            pltpu.VMEM((OWNERS, NPSI, LANES), BF),
            pltpu.VMEM((PAIRS, WIDE), F32),
        ],
        compiler_params=pltpu.CompilerParams(vmem_limit_bytes=24 * MIB),
        cost_estimate=pl.CostEstimate(
            flops=8 * 1024 * MIB, bytes_accessed=4 * MIB, transcendentals=0
        ),
        name="evaluate",
    )(
        visits[0].T,
        core,
        ids,
        mine.reshape(CHIPS * SHARDS, LANES),
        theirs.reshape(CHIPS * SHARDS, LANES),
        jnp.asarray(psi_tables()),
        jnp.asarray(phi_tables()),
        pairs,
        lanes,
        *fields,
    )
    return timeline.reshape(-1)


def solution(mesh):
    placed = (
        P("shard", None, None),
        P("order", None),
        P("shard", "order", None, None),
        P(("order", "shard"), None, None),
        P(("order", "shard")),
        P(("order", "shard")),
        P(("order", "shard")),
        P(None, ("order", "shard")),
    )
    return jax.shard_map(
        shards, mesh=mesh, in_specs=placed, out_specs=P(("order", "shard")), check_vma=False
    )
```

```python
import math

import jax
import jax.numpy as jnp
import numpy as np
from jax import lax
from jax.experimental import pallas as pl
from jax.experimental.pallas import tpu as pltpu
from jax.sharding import PartitionSpec as P

BF = jnp.bfloat16
F32 = jnp.float32
MESH_AXES = ("order", "shard")
NPHI = 4096
NPSI = 128
MODES = 32
ORDERS = 64
GROUPS = 4
SHARDS = 32
OWNERS = 128
LANES = 128
RANKS = 192
WIDE = 256
ITEMS = 4
LOCAL = 16
DEGREES = 2048
REPEAT = 16
CHIPS = 64
PEERS = [[core + 2 * chip for chip in range(CHIPS)] for core in range(2)]
MIB = 1024 * 1024
PAIRS = 64
FIELDS = 8
LOOK = 16
BACK = 8
NT = (((1,), (1,)), ((), ()))


def phi_tables():
    phi = np.arange(NPHI, dtype=np.int64)[:, None]
    mode = np.arange(MODES, dtype=np.int64)[None, :]
    phase = ((phi * mode) % NPHI).astype(np.float64) * (2.0 * math.pi / NPHI)
    both = np.concatenate([np.cos(phase), -np.sin(phase)], axis=1)
    both = both.reshape(NPHI, 2, MODES // 2, 2).transpose(0, 1, 3, 2)
    blocks = both.reshape(NPHI // LANES, LANES, 2 * MODES).transpose(0, 2, 1)
    return blocks.astype(jnp.bfloat16)


def psi_tables():
    psi = np.arange(NPSI, dtype=np.int64)[:, None]
    order = np.arange(ORDERS, dtype=np.int64)[None, :]
    phase = ((psi * order) % NPSI).astype(np.float64) * (2.0 * math.pi / NPSI)
    cos, sin = np.cos(phase), np.sin(phase)
    real = np.stack([cos, -sin], axis=2).reshape(NPSI, 2 * ORDERS)
    imag = np.stack([sin, cos], axis=2).reshape(NPSI, 2 * ORDERS)
    return np.concatenate([real, imag], axis=0).astype(jnp.bfloat16)


def iota_bf(shape, dim):
    return lax.broadcasted_iota(jnp.int32, shape, dim).astype(F32).astype(BF)


def coeff_kernel(
    sky_hbm, beam_hbm, wigner_hbm, out_hbm, sky_ref, beam_ref, wigner, mixed, turned, copies, small, large, outs
):
    half = LOCAL // 2
    first = [
        pltpu.make_async_copy(sky_hbm, sky_ref, small.at[0]),
        pltpu.make_async_copy(beam_hbm, beam_ref, small.at[1]),
    ]
    loads = [
        pltpu.make_async_copy(
            wigner_hbm.at[0, pl.ds(i * half, half)], wigner.at[pl.ds(i * half, half)], large.at[i]
        )
        for i in range(2)
    ]
    for copy in first + loads:
        copy.start()
    for copy in first:
        copy.wait()
    sky = sky_ref[0]
    for i in range(2):
        loads[i].wait()
        for k in range(i * half, (i + 1) * half):
            weighted = (sky * beam_ref[k : k + 1, :]).astype(BF)
            mixed[2 * k : 2 * k + 2, :] = jnp.dot(weighted, wigner[k], preferred_element_type=F32)
    turned[...] = mixed[...].T
    block = jnp.concatenate(
        [turned[pl.ds(row, SHARDS, stride=4), :] for row in range(4)], axis=1
    ).astype(BF)
    for i in range(REPEAT):
        copies[i] = block
    sends = [
        pltpu.make_async_copy(copies, out_hbm.at[pl.ds(i * REPEAT, REPEAT)], outs.at[i])
        for i in range(CHIPS // REPEAT)
    ]
    for copy in sends:
        copy.start()
    for copy in sends:
        copy.wait()


def bucket_kernel(slot_ref, phi_ref, psi_ref, frac_ref, *refs):
    fields, (ids_ref, pair_ref, lane_ref, g_ref, rank_ref, carry, lhs, hot) = refs[:FIELDS], refs[FIELDS:]
    zero = jnp.zeros((), BF)
    one = jnp.ones((), BF)
    own_iota = iota_bf((OWNERS, LANES), 0)
    own_wide = lax.broadcasted_iota(jnp.int32, (OWNERS, LANES), 0)
    rank_iota = iota_bf((RANKS, LANES), 0)
    before = (
        lax.broadcasted_iota(jnp.int32, (LANES, 2 * LANES), 0)
        < lax.broadcasted_iota(jnp.int32, (LANES, 2 * LANES), 1)
    ).astype(F32).astype(BF)
    carry[...] = jnp.zeros_like(carry)
    g_ref[...] = jnp.zeros_like(g_ref)

    def block(step, _):
        start = pl.multiple_of(step * 8, 8)
        slots = slot_ref[pl.ds(start, 8), :]
        owners = slots >> 2
        names = owners.astype(F32)
        rows = ((slots & 3) * 32 + phi_ref[pl.ds(start, 8), :]).astype(F32)
        psis = psi_ref[pl.ds(start, 8), :].astype(F32)
        seen = carry[...]
        ranks = []
        for u in range(8):
            mask = own_iota == names[u : u + 1].astype(BF)
            count = jnp.dot(jnp.where(mask, one, zero), before, preferred_element_type=F32)
            place = count[:, :LANES] + seen
            seen = seen + count[:, LANES:]
            rank = jnp.sum(
                jnp.where(own_wide == owners[u : u + 1], place, 0.0), axis=0, keepdims=True
            )
            ranks.append(rank)
            cut = slice(u * LANES, (u + 1) * LANES)
            hot[:, cut] = jnp.where(rank_iota == rank.astype(BF), one, zero)
            along = pl.ds(pl.multiple_of((start + u) * LANES, LANES), LANES)
            items = (rows[u : u + 1], psis[u : u + 1], frac_ref[0:1, along], frac_ref[1:2, along])
            for n, item in enumerate(items):
                lhs[n * OWNERS : (n + 1) * OWNERS, cut] = jnp.where(mask, item.astype(BF), zero)
        carry[...] = seen
        rank_ref[pl.ds(start, 8), :] = jnp.concatenate(ranks, axis=0)
        g_ref[:, :RANKS] += lax.dot_general(lhs[...], hot[...], NT, preferred_element_type=F32)
        return 0

    lax.fori_loop(0, 16, block, 0, unroll=4)

    square = (OWNERS, OWNERS)
    across = lax.broadcasted_iota(jnp.int32, square, 1).astype(F32)
    down = lax.broadcasted_iota(jnp.int32, square, 0).astype(F32)
    heavy = carry[...] > 128.0
    earlier = jnp.where(across < down, 1.0, 0.0).astype(BF)
    ahead = jnp.dot(
        earlier, jnp.where(heavy, 1.0, 0.0).astype(BF), preferred_element_type=F32
    )
    pair = jnp.where(heavy, ahead, down - ahead)
    here = pair == across
    first = jnp.where(heavy, jnp.where(here, 1.0, 0.0), 0.0)
    second = jnp.where(heavy, 0.0, jnp.where(here, 1.0, 0.0))
    ids_ref[...] = jnp.concatenate(
        [jnp.sum(pick * down, axis=0, keepdims=True) for pick in (first, second)], axis=0
    ).astype(jnp.int32)
    first = first.T[:PAIRS].astype(BF)
    second = second.T[:PAIRS].astype(BF)
    late = lax.broadcasted_iota(jnp.int32, (PAIRS, WIDE), 1) >= RANKS
    merged = []
    for n in range(ITEMS):
        values = g_ref[n * OWNERS : (n + 1) * OWNERS, :].astype(BF)
        long = jnp.dot(first, values, preferred_element_type=F32)
        short = jnp.dot(second, values, preferred_element_type=F32)
        merged.append(jnp.where(late, pltpu.roll(short, RANKS, axis=1), long))
    row, psi, a, b = merged
    row = jnp.where(late, row + 128.0, row)
    fields[0][...] = row
    fields[1][...] = row + 1.0
    fields[2][...] = psi
    fields[3][...] = jnp.where(psi == NPSI - 1.0, 0.0, psi + 1.0)
    fields[4][...] = 1.0 - a
    fields[5][...] = a
    fields[6][...] = 1.0 - b
    fields[7][...] = b
    lane_ref[...] = jnp.where(heavy, pair, pair + 64.0)

    def address(step, code):
        start = pl.multiple_of(step * 8, 8)
        owners = slot_ref[pl.ds(start, 8), :] >> 2
        found = jnp.concatenate(
            [
                jnp.sum(
                    jnp.where(own_wide == owners[u : u + 1], code[...], 0.0), axis=0, keepdims=True
                )
                for u in range(8)
            ],
            axis=0,
        )
        light = found >= 64.0
        pair_ref[pl.ds(start, 8), :] = jnp.where(light, found - 64.0, found)
        rank_ref[pl.ds(start, 8), :] += jnp.where(light, 1.0 * RANKS, 0.0)
        return code

    carry[...] = lane_ref[...]
    lax.fori_loop(0, 16, lambda step, _: (address(step, carry), 0)[1], 0, unroll=2)
    lane_ref[...] = rank_ref[...]


def eval_kernel(
    visits_ref,
    core_ref,
    ids_ref,
    mine_ref,
    theirs_ref,
    w_ref,
    phi_ref,
    pair_ref,
    lane_ref,
    *refs,
):
    fields, (out_ref, coeff, spec, tile_ref, found) = refs[:FIELDS], refs[FIELDS:]
    zero = jnp.zeros((), BF)
    one = jnp.ones((), BF)
    lane = lax.broadcasted_iota(jnp.int32, (1, LANES), 1) // 32

    for i, narrow in enumerate((mine_ref, theirs_ref)):
        side = core_ref[0] ^ i

        def widen(step, _):
            source = pl.multiple_of(step * 256, 256)
            place = (step // 2) * 4 + side * 2 + step % 2
            target = pl.multiple_of(place * 256, 256)
            coeff[pl.ds(target, 256), :] = narrow[pl.ds(source, 256), :].astype(F32)
            return 0

        lax.fori_loop(0, 8, widen, 0, unroll=2)

    def spectrum(pair):
        blocks = []
        for v in range(2):
            block = coeff[pl.ds(pair * 2 + v, LANES, stride=SHARDS), :]
            turned = [block] + [pltpu.roll(block, 32 * n, axis=1) for n in (1, 2, 3)]
            for row in range(4):
                part = None
                for o in range(4):
                    piece = turned[(o - row) % 4][o * 32 : (o + 1) * 32]
                    part = piece if part is None else jnp.where(lane == o, piece, part)
                blocks.append(part.astype(BF))
        block = jnp.concatenate(blocks, axis=0)
        both = lax.dot_general(w_ref[...], block, NT, preferred_element_type=F32).astype(BF)
        for v in range(2):
            cut = both[:, v * LANES : (v + 1) * LANES]
            spec[pair * 2 + v] = jnp.concatenate([cut[:NPSI], cut[NPSI:]], axis=1)

    def tiles(s):
        source = spec[s]
        for pair in range(2):
            chosen = []
            for o in (2 * pair, 2 * pair + 1):
                waves, lane_row = None, None
                for j in range(4):
                    tile = jnp.maximum(visits_ref[j, o * SHARDS + s], 0)
                    turn_by = ((j - tile) & 3) * 32
                    wave = pltpu.roll(phi_ref[o * 8 + ((tile & 31) >> 2)], turn_by, axis=1)
                    row = jnp.full((1, LANES), tile >> 5, jnp.int32)
                    waves = wave if j == 0 else jnp.where(lane == j, wave, waves)
                    lane_row = row if j == 0 else jnp.where(lane == j, row, lane_row)
                chosen.append(
                    jnp.concatenate(
                        [
                            jnp.where(lane_row == row, waves[c * 32 : (c + 1) * 32], zero)
                            for c in range(2)
                            for row in range(4)
                        ],
                        axis=0,
                    )
                )
            cells = jnp.dot(source, jnp.concatenate(chosen, axis=1), preferred_element_type=F32)
            for v in range(2):
                tile_ref[(2 * pair + v) * SHARDS + s] = cells[:, v * LANES : (v + 1) * LANES].astype(BF)

    def turn(pair, _):
        for v in range(2):
            tiles((pair - 1) * 2 + v)
        spectrum(pair)
        return 0

    spectrum(0)
    lax.fori_loop(1, SHARDS // 2, turn, 0, unroll=15)
    for v in range(2):
        tiles(SHARDS - 2 + v)

    near = iota_bf((LANES, WIDE), 0)
    far = near[:, LANES:] + jnp.asarray(128.0, BF)
    empty = jnp.zeros((LANES, LANES), BF)

    def look(step, _):
        for u in range(LOOK):
            p = step * LOOK + u
            row0, row1, q0, q1, a0, a1, b0, b1 = [
                field[pl.ds(p, 1), :].astype(BF) for field in fields
            ]
            top = jnp.where(near == row0, a0, jnp.where(near == row1, a1, zero))
            low = jnp.where(
                far == row0[:, LANES:],
                a0[:, LANES:],
                jnp.where(far == row1[:, LANES:], a1[:, LANES:], zero),
            )
            hot = jnp.concatenate([top, jnp.concatenate([empty, low], axis=1)], axis=0)
            both = jnp.concatenate([tile_ref[ids_ref[0, p]], tile_ref[ids_ref[1, p]]], axis=1)
            seen = jnp.dot(both, hot, preferred_element_type=F32)
            weight = jnp.where(near == q0, b0, jnp.where(near == q1, b1, zero))
            found[pl.ds(p, 1), :] = jnp.sum(seen * weight.astype(F32), axis=0, keepdims=True)
        return 0

    lax.fori_loop(0, PAIRS // LOOK, look, 0)

    lane_iota = iota_bf((WIDE, LANES), 0)
    pair_iota = iota_bf((PAIRS, LANES), 0)

    def back(step, values):
        start = pl.multiple_of(step * 8, 8)
        pairs = pair_ref[pl.ds(start, 8), :]
        lanes = lane_ref[pl.ds(start, 8), :]
        result = []
        for u in range(0, 8, 2):
            hot = jnp.concatenate(
                [
                    jnp.where(lane_iota == lanes[v : v + 1].astype(BF), one, zero)
                    for v in (u, u + 1)
                ],
                axis=1,
            )
            moved = jnp.dot(values, hot, preferred_element_type=F32).astype(BF)
            for v in (u, u + 1):
                part = moved[:, (v - u) * LANES : (v - u + 1) * LANES]
                part = jnp.where(pair_iota == pairs[v : v + 1].astype(BF), part, zero)
                part = part[:32] + part[32:]
                part = (part[:16] + part[16:]).astype(F32)
                result.append(jnp.sum(part, axis=0, keepdims=True))
        out_ref[pl.ds(start, 8), :] = jnp.concatenate(result, axis=0)
        return values

    lax.fori_loop(0, 16, back, found[...].astype(BF), unroll=BACK)


def shards(sky_coeffs, beam_coeffs, wigner, visits, point_slot, phi_cell, psi_cell, fraction):
    vmem = pl.BlockSpec(memory_space=pltpu.VMEM)
    anywhere = pl.BlockSpec(memory_space=pl.ANY)
    dma = pltpu.SemaphoreType.DMA
    copies = pl.pallas_call(
        coeff_kernel,
        out_shape=jax.ShapeDtypeStruct((CHIPS, SHARDS, LANES), BF),
        in_specs=[anywhere] * 3,
        out_specs=anywhere,
        scratch_shapes=[
            pltpu.VMEM((1, 2, DEGREES), F32),
            pltpu.VMEM((LOCAL, DEGREES), F32),
            pltpu.VMEM((LOCAL, DEGREES, LANES), BF),
            pltpu.VMEM((2 * LOCAL, LANES), F32),
            pltpu.VMEM((LANES, 2 * LOCAL), F32),
            pltpu.VMEM((REPEAT, SHARDS, LANES), BF),
            dma((2,)),
            dma((2,)),
            dma((CHIPS // REPEAT,)),
        ],
        compiler_params=pltpu.CompilerParams(vmem_limit_bytes=60 * MIB),
        cost_estimate=pl.CostEstimate(
            flops=16 * MIB, bytes_accessed=9 * MIB, transcendentals=0
        ),
        name="coeffs",
    )(sky_coeffs, beam_coeffs, wigner)
    mine = lax.all_to_all(copies, MESH_AXES, 0, 0, axis_index_groups=PEERS, tiled=True)
    core = jnp.full((1,), lax.axis_index("shard") & 1, jnp.int32)
    slots = point_slot.reshape(OWNERS, LANES)
    table = jax.ShapeDtypeStruct((OWNERS, LANES), F32)
    *fields, ids, pairs, lanes = pl.pallas_call(
        bucket_kernel,
        out_shape=[jax.ShapeDtypeStruct((PAIRS, WIDE), F32)] * FIELDS
        + [jax.ShapeDtypeStruct((2, OWNERS), jnp.int32), table, table],
        in_specs=[vmem] * 4,
        out_specs=[vmem] * (FIELDS + 3),
        scratch_shapes=[
            pltpu.VMEM((ITEMS * OWNERS, WIDE), F32),
            pltpu.VMEM((OWNERS, LANES), F32),
            pltpu.VMEM((OWNERS, LANES), F32),
            pltpu.VMEM((ITEMS * OWNERS, 8 * LANES), BF),
            pltpu.VMEM((RANKS, 8 * LANES), BF),
        ],
        compiler_params=pltpu.CompilerParams(vmem_limit_bytes=12 * MIB),
        cost_estimate=pl.CostEstimate(
            flops=8 * 1024 * MIB, bytes_accessed=2 * MIB, transcendentals=0
        ),
        name="bucket",
    )(slots, phi_cell.reshape(OWNERS, LANES), psi_cell.reshape(OWNERS, LANES), fraction)
    mine, lanes = lax.optimization_barrier((mine, lanes))
    theirs = lax.ppermute(mine, "shard", [(n, n ^ 1) for n in range(SHARDS)])
    timeline = pl.pallas_call(
        eval_kernel,
        out_shape=jax.ShapeDtypeStruct((OWNERS, LANES), F32),
        in_specs=[pl.BlockSpec(memory_space=pltpu.SMEM)] * 3 + [vmem] * (6 + FIELDS),
        out_specs=vmem,
        scratch_shapes=[
            pltpu.VMEM((OWNERS * SHARDS, LANES), F32),
            pltpu.VMEM((SHARDS, NPSI, 2 * LANES), BF),
            pltpu.VMEM((OWNERS, NPSI, LANES), BF),
            pltpu.VMEM((PAIRS, WIDE), F32),
        ],
        compiler_params=pltpu.CompilerParams(vmem_limit_bytes=24 * MIB),
        cost_estimate=pl.CostEstimate(
            flops=8 * 1024 * MIB, bytes_accessed=4 * MIB, transcendentals=0
        ),
        name="evaluate",
    )(
        visits[0].T,
        core,
        ids,
        mine.reshape(CHIPS * SHARDS, LANES),
        theirs.reshape(CHIPS * SHARDS, LANES),
        jnp.asarray(psi_tables()),
        jnp.asarray(phi_tables()),
        pairs,
        lanes,
        *fields,
    )
    return timeline.reshape(-1)


def solution(mesh):
    placed = (
        P("shard", None, None),
        P("order", None),
        P("shard", "order", None, None),
        P(("order", "shard"), None, None),
        P(("order", "shard")),
        P(("order", "shard")),
        P(("order", "shard")),
        P(None, ("order", "shard")),
    )
    return jax.shard_map(
        shards, mesh=mesh, in_specs=placed, out_specs=P(("order", "shard")), check_vma=False
    )
```
